32 devices in a mesh: ctx: 16 (over z, x, core), ch: 2 (over y).
Axes of the slice: x: 2, y: 2, z: 4, core: 2. Of those that a mesh axis runs over, the one named last changes fastest.
Arguments:
- grad_out: bfloat16 [2048, 4096], P('ctx', 'ch'), may hold values from -6 to 6
- inputs: bfloat16 [2048, 4096], P('ctx', 'ch'), may hold values from -0.3125 to 0.3125
- filter_taps: bfloat16 [128, 8, 4096], P('ctx', 'ch'), may hold values from -0.1875 to 0.1875
Outputs:
- grad_inputs: bfloat16 [2048, 4096], P('ctx', 'ch')
- grad_taps: float32 [128, 8, 4096], P('ctx', 'ch')
The draws below stay inside these ranges and needn't reach their ends.
All inputs are finite; a program needn't handle non-finite values.
Results may differ from the reference program's by a relative error of at most 0.0085.
Values may be sent and summed in bfloat16 or wider, within the bound.
No kernel may reach another device: no remote copies, remote signals or barrier semaphores. Data moves between devices by JAX's collectives and lax.ppermute only.
A program may use at most 128 MiB of HBM per device.

```python
import math
import jax
import jax.numpy as jnp
from jax import lax

D = 4096
TOK_DEV = 128
FILT_DEVS = 8
FILT_LEN = 1024
SEQ_LEN = 2048
TOKENS = 2048


def steps_of(key, dims, pieces, least, top_value):
    level, own = 1.0, jax.random.fold_in(key, 6)
    for axis_at, parts in pieces:
        draws = jnp.exp(jax.random.uniform(jax.random.fold_in(own, axis_at), (parts,), jnp.float32, least / len(pieces), top_value / len(pieces)))
        level = level * jnp.repeat(draws, dims[axis_at] // parts).reshape([-1 if axis == axis_at else 1 for axis in range(len(dims))])
    return level


def bell_draw(rng, dims, scale, limit, pieces=(), kind=jnp.bfloat16):
    entries = scale * jax.random.normal(rng, dims, jnp.float32)
    if pieces:
        entries = entries * steps_of(rng, dims, pieces, -0.22, 0.18)
    return jnp.clip(entries, -limit, limit).astype(kind)


def setup_inputs(seed: int = 0) -> dict:
    key_list = jax.random.split(jax.random.key(seed), 4)
    grad_out = bell_draw(key_list[0], (TOKENS, D), 1.0, 6.0, ((0, 16), (1, 2)))
    inputs = bell_draw(key_list[1], (TOKENS, D), (1 / SEQ_LEN ** 0.5), 0.3125, ((0, 16), (1, 2)))
    filter_taps = bell_draw(key_list[2], (TOK_DEV, FILT_DEVS, D), FILT_LEN ** -0.5, 0.1875, ((0, 16), (1, 2)))
    return {"grad_out": grad_out, "inputs": inputs, "filter_taps": filter_taps}


def reference(grad_out, inputs, filter_taps):
    length = SEQ_LEN
    padded_len = 2 * length
    col_block = math.gcd(D, 256)
    col_count = D // col_block
    filter_full = jnp.transpose(filter_taps.astype(jnp.float32), (1, 0, 2)).reshape(FILT_LEN, col_count, col_block)
    filter_cols = jnp.transpose(filter_full, (1, 0, 2))
    grad_cols = jnp.transpose(grad_out.reshape(length, col_count, col_block), (1, 0, 2))
    value_cols = jnp.transpose(inputs.reshape(length, col_count, col_block), (1, 0, 2))

    def one_block(triple):
        filt_block, grad_block, value_block = triple
        filter_spec = jnp.fft.rfft(filt_block, n=padded_len, axis=0)
        grad_spec = jnp.fft.rfft(grad_block.astype(jnp.float32), n=padded_len, axis=0)
        value_spec = jnp.fft.rfft(value_block.astype(jnp.float32), n=padded_len, axis=0)
        grad_in = jnp.fft.irfft(jnp.conj(filter_spec) * grad_spec, n=padded_len, axis=0)[:length]
        tap_term = jnp.fft.irfft(grad_spec * jnp.conj(value_spec), n=padded_len, axis=0)[:FILT_LEN]
        return grad_in.astype(jnp.bfloat16), tap_term.astype(filt_block.dtype)

    grad_in, tap_total = lax.map(one_block, (filter_cols, grad_cols, value_cols))
    grad_inputs = jnp.transpose(grad_in, (1, 0, 2)).reshape(length, D)
    tap_full = jnp.transpose(tap_total, (1, 0, 2)).reshape(FILT_DEVS, TOK_DEV, D)
    grad_taps = jnp.transpose(tap_full, (1, 0, 2))
    return grad_inputs, grad_taps
```

```python
import functools

import jax
import jax.numpy as jnp
import numpy as np
from jax import lax
from jax.experimental import pallas as pl
from jax.experimental.pallas import tpu as pltpu
from jax.sharding import PartitionSpec as P

F32 = jnp.float32
BF16 = jnp.bfloat16


def two_bf16(table):
    upper = table.astype(np.float32).astype(jnp.bfloat16)
    lower = (table - upper.astype(np.float64)).astype(np.float32).astype(jnp.bfloat16)
    return upper, lower


def dft_tables(block):
    freq = np.concatenate([np.arange(0, block, 2), np.arange(1, block, 2)])
    turns = ((2 * freq[:, None] + 1) * np.arange(block)[None, :]) % (4 * block)
    angle = turns * (np.pi / (2 * block))
    forward = np.concatenate([np.cos(angle), -np.sin(angle)], 0)
    return two_bf16(forward) + two_bf16(forward.T / block)


def forward_dft(tables, block, columns):
    upper, lower = tables
    first = jnp.dot(upper[...], columns, preferred_element_type=F32)
    return first + jnp.dot(lower[...], columns, preferred_element_type=F32)


def inverse_dft(tables, spec):
    upper, lower = tables
    head = spec.astype(BF16)
    tail = (spec - head.astype(F32)).astype(BF16)
    total = jnp.dot(upper[...], head, preferred_element_type=F32)
    total += jnp.dot(lower[...], head, preferred_element_type=F32)
    return total + jnp.dot(upper[...], tail, preferred_element_type=F32)


def side_by_side(width):
    return 2 if width % 128 == 0 else 1


def spectra(tables, block, rows_ref, spec_ref):
    count, _, width = spec_ref.shape
    group = side_by_side(width)
    for j in range(0, count, group):
        parts = [rows_ref[pl.ds((j + u) * block, block), :] for u in range(group)]
        both = forward_dft(tables, block, jnp.concatenate(parts, 1) if group > 1 else parts[0])
        for u in range(group):
            spec_ref[j + u] = both[:, u * width : (u + 1) * width]


def windows(block, spec_ref, window_ref):
    count = spec_ref.shape[0]
    half = block // 2
    for j in range(count):
        if j + 1 == count:
            window_ref[j] = spec_ref[j]
            continue
        for start, sign in ((0, 1), (half, -1)):
            real, imag = pl.ds(start, half), pl.ds(block + start, half)
            next_imag, next_real = spec_ref[j + 1, imag], spec_ref[j + 1, real]
            if sign > 0:
                window_ref[j, real] = spec_ref[j, real] + next_imag
                window_ref[j, imag] = spec_ref[j, imag] - next_real
            else:
                window_ref[j, real] = spec_ref[j, real] - next_imag
                window_ref[j, imag] = spec_ref[j, imag] + next_real


def correlate(block, left_ref, window_ref, out_ref):
    lefts, outs, count = left_ref.shape[0], out_ref.shape[0], window_ref.shape[0]

    def body(t, carry):
        real = pl.ds(pl.multiple_of(t * 8, 8), 8)
        imag = pl.ds(pl.multiple_of(block + t * 8, 8), 8)
        for a in range(outs):
            sum_real = sum_imag = None
            for s in range(min(lefts, count - a)):
                lr, li = left_ref[s, real], left_ref[s, imag]
                wr, wi = window_ref[a + s, real], window_ref[a + s, imag]
                re = lr * wr + li * wi
                im = lr * wi - li * wr
                sum_real = re if sum_real is None else sum_real + re
                sum_imag = im if sum_imag is None else sum_imag + im
            out_ref[a, real] = sum_real
            out_ref[a, imag] = sum_imag
        return carry

    lax.fori_loop(0, block // 8, body, 0)


def invert(tables, block, spec_ref, out_ref):
    count, _, width = spec_ref.shape
    group = side_by_side(width)
    for j in range(0, count, group):
        parts = [spec_ref[j + u] for u in range(group)]
        both = inverse_dft(tables, jnp.concatenate(parts, 1) if group > 1 else parts[0])
        for u in range(group):
            out_ref[pl.ds((j + u) * block, block), :] = both[
                :, u * width : (u + 1) * width
            ].astype(out_ref.dtype)


def input_grad_kernel(block, grad_ref, taps_ref, fu, fl, iu, il, out_ref, window_ref, spec, tap_spec):
    spectra((fu, fl), block, grad_ref, spec)
    windows(block, spec, window_ref)
    spectra((fu, fl), block, taps_ref, tap_spec)
    correlate(block, tap_spec, window_ref, spec)
    invert((iu, il), block, spec, out_ref)


def tap_grad_kernel(block, value_ref, window_ref, fu, fl, iu, il, out_ref, spec, tap_spec):
    spectra((fu, fl), block, value_ref, spec)
    correlate(block, spec, window_ref, tap_spec)
    invert((iu, il), block, tap_spec, out_ref)


def call_kernel(body, out_shape, scratch, operands, flops):
    padded = sum(
        int(np.prod(a.shape[:-1])) * max(a.shape[-1], 128) * 4
        for a in list(operands) + list(out_shape) + list(scratch)
    )
    moved = sum(int(np.prod(a.shape)) * a.dtype.itemsize for a in list(operands) + list(out_shape))
    return pl.pallas_call(
        body,
        out_shape=out_shape,
        in_specs=[pl.BlockSpec(memory_space=pltpu.VMEM)] * len(operands),
        out_specs=[pl.BlockSpec(memory_space=pltpu.VMEM)] * len(out_shape),
        scratch_shapes=[pltpu.VMEM(a.shape, a.dtype) for a in scratch],
        compiler_params=pltpu.CompilerParams(vmem_limit_bytes=min(padded + (8 << 20), 56 << 20)),
        cost_estimate=pl.CostEstimate(flops=flops, bytes_accessed=moved, transcendentals=0),
    )(*operands)


def shards(grad_out, inputs, filter_taps):
    rows, width = grad_out.shape
    ctx, ch = lax.axis_size("ctx"), lax.axis_size("ch")
    tap_rows, tap_segs, channels = filter_taps.shape
    own = width // ctx
    block = 2 * rows
    length = rows * ctx
    taps = rows * tap_segs * ch
    shape = jax.ShapeDtypeStruct

    def to_channels(array):
        parts = array.reshape(rows, ctx, own).transpose(1, 0, 2)
        return lax.all_to_all(parts, "ctx", 0, 0, tiled=True).reshape(length, own)

    grad = to_channels(grad_out)
    tap_parts = filter_taps.reshape(tap_rows, tap_segs, ch, ctx, own).transpose(3, 2, 0, 1, 4)
    tap_parts = tap_parts.reshape(ctx * ch, tap_rows, tap_segs, own)
    tap_parts = lax.all_to_all(tap_parts, ("ctx", "ch"), 0, 0, tiled=True)
    tap_all = tap_parts.reshape(ctx, ch, tap_rows, tap_segs, own).transpose(1, 3, 0, 2, 4)
    tap_all = tap_all.reshape(taps, own)
    value = to_channels(inputs)

    tables = tuple(jnp.asarray(t) for t in dft_tables(block))
    blocks, tap_blocks = length // block, taps // block
    spec = shape((blocks, 2 * block, own), F32)
    tap_spec = shape((tap_blocks, 2 * block, own), F32)
    flops = 2 * 2 * block * block * own * (blocks * 5 + tap_blocks * 2)
    input_grad, window = call_kernel(
        functools.partial(input_grad_kernel, block),
        [shape((length, own), BF16), spec],
        [spec, tap_spec],
        (grad, tap_all) + tables,
        flops,
    )
    (tap_grad,) = call_kernel(
        functools.partial(tap_grad_kernel, block),
        [shape((taps, own), BF16)],
        [spec, tap_spec],
        (value, window) + tables,
        flops,
    )

    back = lax.all_to_all(input_grad.reshape(ctx, rows, own), "ctx", 0, 0, tiled=True)
    grad_inputs = back.transpose(1, 0, 2).reshape(rows, width)
    out_parts = tap_grad.reshape(ch, tap_segs, ctx, tap_rows, own).transpose(2, 0, 3, 1, 4)
    out_parts = out_parts.reshape(ctx * ch, tap_rows, tap_segs, own)
    out_parts = lax.all_to_all(out_parts, ("ctx", "ch"), 0, 0, tiled=True)
    out_parts = out_parts.reshape(ctx, ch, tap_rows, tap_segs, own).transpose(2, 3, 1, 0, 4)
    grad_taps = out_parts.reshape(tap_rows, tap_segs, channels).astype(F32)
    return grad_inputs, grad_taps


def solution(mesh):
    return jax.shard_map(
        shards,
        mesh=mesh,
        in_specs=(P("ctx", "ch"), P("ctx", "ch"), P("ctx", "ch", None)),
        out_specs=(P("ctx", "ch"), P("ctx", "ch", None)),
        check_vma=False,
    )
```

```python
import functools

import jax
import jax.numpy as jnp
import numpy as np
from jax import lax
from jax.experimental import pallas as pl
from jax.experimental.pallas import tpu as pltpu
from jax.sharding import PartitionSpec as P

F32 = jnp.float32
BF16 = jnp.bfloat16


def two_bf16(table):
    upper = table.astype(np.float32).astype(jnp.bfloat16)
    lower = (table - upper.astype(np.float64)).astype(np.float32).astype(jnp.bfloat16)
    return np.stack([upper, lower])


def dft_tables(block):
    freq = np.concatenate([np.arange(0, block, 2), np.arange(1, block, 2)])
    turns = ((2 * freq[:, None] + 1) * np.arange(block)[None, :]) % (4 * block)
    angle = turns * (np.pi / (2 * block))
    forward = np.concatenate([np.cos(angle), -np.sin(angle)], 0)
    return two_bf16(forward), two_bf16(forward.T / block)


def forward_dft(tables, block, columns):
    upper, lower = tables
    first = jnp.dot(upper[...], columns, preferred_element_type=F32)
    return first + jnp.dot(lower[...], columns, preferred_element_type=F32)


def inverse_dft(tables, spec):
    upper, lower = tables
    head = spec.astype(BF16)
    tail = (spec - head.astype(F32)).astype(BF16)
    total = jnp.dot(upper[...], head, preferred_element_type=F32)
    total += jnp.dot(lower[...], head, preferred_element_type=F32)
    return total + jnp.dot(upper[...], tail, preferred_element_type=F32)


def side_by_side(width):
    return 2 if width % 128 == 0 else 1


def spectra(tables, block, load, spec_ref):
    count, _, width = spec_ref.shape
    group = side_by_side(width)
    for j in range(0, count, group):
        parts = [load(j + u) for u in range(group)]
        both = forward_dft(tables, block, jnp.concatenate(parts, 1) if group > 1 else parts[0])
        for u in range(group):
            spec_ref[j + u] = both[:, u * width : (u + 1) * width]


def windows(block, spec_ref, window_ref):
    count = spec_ref.shape[0]
    half = block // 2
    for j in range(count):
        if j + 1 == count:
            window_ref[j] = spec_ref[j]
            continue
        for start, sign in ((0, 1), (half, -1)):
            real, imag = pl.ds(start, half), pl.ds(block + start, half)
            next_imag, next_real = spec_ref[j + 1, imag], spec_ref[j + 1, real]
            if sign > 0:
                window_ref[j, real] = spec_ref[j, real] + next_imag
                window_ref[j, imag] = spec_ref[j, imag] - next_real
            else:
                window_ref[j, real] = spec_ref[j, real] - next_imag
                window_ref[j, imag] = spec_ref[j, imag] + next_real


def correlate(block, left_ref, window_ref, out_ref):
    lefts, outs, count = left_ref.shape[0], out_ref.shape[0], window_ref.shape[0]

    def body(t, carry):
        real = pl.ds(pl.multiple_of(t * 8, 8), 8)
        imag = pl.ds(pl.multiple_of(block + t * 8, 8), 8)
        for a in range(outs):
            sum_real = sum_imag = None
            for s in range(min(lefts, count - a)):
                lr, li = left_ref[s, real], left_ref[s, imag]
                wr, wi = window_ref[a + s, real], window_ref[a + s, imag]
                re = lr * wr + li * wi
                im = lr * wi - li * wr
                sum_real = re if sum_real is None else sum_real + re
                sum_imag = im if sum_imag is None else sum_imag + im
            out_ref[a, real] = sum_real
            out_ref[a, imag] = sum_imag
        return carry

    lax.fori_loop(0, block // 8, body, 0)


def invert(tables, block, spec_ref, store):
    count, _, width = spec_ref.shape
    group = side_by_side(width)
    for j in range(0, count, group):
        parts = [spec_ref[j + u] for u in range(group)]
        both = inverse_dft(tables, jnp.concatenate(parts, 1) if group > 1 else parts[0])
        for u in range(group):
            store(j + u, both[:, u * width : (u + 1) * width].astype(BF16))


def fetch(pairs, sems):
    copies = [pltpu.make_async_copy(far, near, sems.at[k]) for k, (far, near) in enumerate(pairs)]
    for copy in copies:
        copy.start()
    return copies


def half_of(ref, rows, half):
    def load(j):
        return jnp.concatenate([ref[2 * j + u, pl.ds(half * rows, rows), :] for u in range(2)], 0)

    return load


def both_grads(block, loads, stores, refs):
    forward, inverse, fv, iv, spec, window, tap_spec, tap_sum, sems = refs
    copies = fetch([(forward, fv), (inverse, iv)], sems)
    load_grad, load_value, load_taps = loads()
    ahead, back = (fv.at[0], fv.at[1]), (iv.at[0], iv.at[1])
    copies[0].wait()
    spectra(ahead, block, load_grad, spec)
    windows(block, spec, window)
    spectra(ahead, block, load_value, spec)
    correlate(block, spec, window, tap_sum)
    spectra(ahead, block, load_taps, tap_spec)
    correlate(block, tap_spec, window, spec)
    copies[1].wait()
    invert(back, block, tap_sum, stores[1])
    invert(back, block, spec, stores[0])


def plain_kernel(block, sent_ref, taps_ref, forward, inverse, grad_ref, tap_grad_ref, *refs):
    rows = block // 2

    def loads():
        return (
            half_of(sent_ref, rows, 0),
            half_of(sent_ref, rows, 1),
            lambda j: taps_ref[pl.ds(j * block, block), :],
        )

    def store_grad(j, result):
        for u in range(2):
            grad_ref[2 * j + u] = result[u * rows : (u + 1) * rows]

    def store_taps(j, result):
        tap_grad_ref[pl.ds(j * block, block), :] = result

    both_grads(block, loads, (store_grad, store_taps), (forward, inverse, *refs))


def traded(top, bottom):
    half = top.shape[1] // 2
    left = lax.broadcasted_iota(jnp.int32, top.shape, 1) < half
    return (
        jnp.where(left, top, pltpu.roll(bottom, half, 1)),
        jnp.where(left, pltpu.roll(top, half, 1), bottom),
    )


def pack_kernel(grad_ref, value_ref, taps_ref, out_ref):
    half = grad_ref.shape[0] // 2
    own, size = out_ref.shape[2], taps_ref.shape[2]
    for i in range(out_ref.shape[0] // 2):
        columns = pl.ds(i * own, own)
        for n, ref in enumerate((grad_ref, value_ref)):
            pair = traded(ref[pl.ds(0, half), columns].astype(F32), ref[pl.ds(half, half), columns].astype(F32))
            for j in range(2):
                out_ref[2 * i + j, pl.ds(n * half, half), :] = pair[j].astype(BF16)
        pair = traded(taps_ref[0, i].astype(F32), taps_ref[1, i].astype(F32))
        for j in range(2):
            out_ref[2 * i + j, pl.ds(2 * half, size), :] = pair[j].astype(BF16)


def paired_kernel(sizes, sent_ref, forward, inverse, out_ref, whole, taps, *refs):
    block, tap_rows, tap_segs = sizes
    rows, half = block // 2, block // 4
    count = sent_ref.shape[0] // 2
    size = tap_rows * tap_segs

    def loads():
        for i in range(count):
            for n in range(2):
                pair = [sent_ref[2 * i + j, pl.ds(n * half, half), :].astype(F32) for j in range(2)]
                for u, part in enumerate(traded(*pair)):
                    whole[n, pl.ds(i * rows + u * half, half), :] = part.astype(BF16)
            for j in range(2):
                piece = sent_ref[2 * i + j, pl.ds(2 * half, size), :].astype(F32)
                for s in range(tap_segs):
                    taps[j * tap_segs + s, pl.ds(i * tap_rows, tap_rows), :] = piece[s * tap_rows : (s + 1) * tap_rows]
        return (
            lambda j: whole[0, pl.ds(j * block, block), :],
            lambda j: whole[1, pl.ds(j * block, block), :],
            lambda j: jnp.concatenate([taps[2 * j + u].astype(BF16) for u in range(2)], 0),
        )

    def store_grad(j, result):
        for u in range(2):
            at = u * rows
            result32 = result.astype(F32)
            pair = traded(result32[at : at + half], result32[at + half : at + rows])
            for side in range(2):
                out_ref[2 * (2 * j + u) + side, pl.ds(0, half), :] = pair[side].astype(BF16)

    def store_taps(j, result):
        for u in range(2):
            taps[2 * j + u] = result[u * rows : (u + 1) * rows].astype(F32)
        if 2 * j + 2 < taps.shape[0]:
            return
        for i in range(count):
            for side in range(2):
                pieces = [taps[side * tap_segs + s, pl.ds(i * tap_rows, tap_rows), :] for s in range(tap_segs)]
                out_ref[2 * i + side, pl.ds(half, size), :] = jnp.concatenate(pieces, 0).astype(BF16)

    both_grads(block, loads, (store_grad, store_taps), (forward, inverse, *refs))


def unpack_kernel(sizes, back_ref, grad_ref, taps_ref):
    tap_rows, tap_segs = sizes
    rows, width = grad_ref.shape
    half, own = rows // 2, back_ref.shape[2]
    size = tap_rows * tap_segs
    for i in range(back_ref.shape[0] // 2):
        pair = traded(*[back_ref[2 * i + j, pl.ds(0, half), :].astype(F32) for j in range(2)])
        for u in range(2):
            grad_ref[pl.ds(u * half, half), pl.ds(i * own, own)] = pair[u].astype(BF16)
        pair = traded(*[back_ref[2 * i + j, pl.ds(half, size), :].astype(F32) for j in range(2)])
        for side in range(2):
            for s in range(tap_segs):
                taps_ref[:, s, pl.ds(side * width + i * own, own)] = pair[side][s * tap_rows : (s + 1) * tap_rows]


def split_kernel(*refs):
    ins, out_ref = refs[:-1], refs[-1]
    count, size, own = out_ref.shape
    rows = size // len(ins)
    for k in range(count):
        for n, ref in enumerate(ins):
            out_ref[k, pl.ds(n * rows, rows), :] = ref[:, k * own : (k + 1) * own]


def call_kernel(body, out_shape, operands, scratch=(), flops=0, far=(), sems=0):
    held = [a for k, a in enumerate(operands) if k not in far]
    held += list(out_shape) + list(scratch)
    padded = sum(int(np.prod(a.shape[:-1])) * max(a.shape[-1], 128) * a.dtype.itemsize for a in held)
    moved = sum(int(np.prod(a.shape)) * a.dtype.itemsize for a in list(operands) + list(out_shape))
    near, away = pl.BlockSpec(memory_space=pltpu.VMEM), pl.BlockSpec(memory_space=pl.ANY)
    scratch_shapes = [pltpu.VMEM(a.shape, a.dtype) for a in scratch]
    if sems:
        scratch_shapes.append(pltpu.SemaphoreType.DMA((sems,)))
    return pl.pallas_call(
        body,
        out_shape=out_shape,
        in_specs=[away if k in far else near for k in range(len(operands))],
        out_specs=[near] * len(out_shape),
        scratch_shapes=scratch_shapes,
        compiler_params=pltpu.CompilerParams(vmem_limit_bytes=min(padded + (6 << 20), 56 << 20)),
        cost_estimate=pl.CostEstimate(flops=flops, bytes_accessed=moved, transcendentals=0),
    )(*operands)


def shards(grad_out, inputs, filter_taps):
    rows, width = grad_out.shape
    ctx, ch = lax.axis_size("ctx"), lax.axis_size("ch")
    tap_rows, tap_segs, channels = filter_taps.shape
    own = width // ctx
    block = 2 * rows
    taps = rows * tap_segs * ch
    size = tap_rows * tap_segs
    blocks, tap_blocks = rows * ctx // block, taps // block
    shape = jax.ShapeDtypeStruct
    paired = own == 128 and ch == 2 and rows % 32 == 0 and tap_rows % 8 == 0 and size % 16 == 0

    forward, inverse = (jnp.asarray(t) for t in dft_tables(block))
    spec = shape((blocks, 2 * block, own), F32)
    tap_spec = shape((tap_blocks, 2 * block, own), F32)
    scratch = [shape(forward.shape, BF16), shape(inverse.shape, BF16), spec, spec, tap_spec, tap_spec]
    flops = 4 * block * block * own * 5 * (blocks + tap_blocks)
    tap_parts = filter_taps.reshape(tap_rows, tap_segs, ch, ctx, own)

    if paired:
        tap_parts = tap_parts.transpose(2, 3, 1, 0, 4).reshape(ch, ctx, size, own)
        (sent,) = call_kernel(
            pack_kernel, [shape((ctx * ch, rows + size, own), BF16)], (grad_out, inputs, tap_parts)
        )
        sent = lax.all_to_all(sent, ("ctx", "ch"), 0, 0, tiled=True)
        (back,) = call_kernel(
            functools.partial(paired_kernel, (block, tap_rows, tap_segs)),
            [shape((ctx * ch, rows // 2 + size, own), BF16)],
            (sent, forward, inverse),
            [shape((2, rows * ctx, own), BF16), shape((ch * tap_segs, rows, own), F32)] + scratch,
            flops,
            (1, 2),
            sems=2,
        )
        back = lax.all_to_all(back, ("ctx", "ch"), 0, 0, tiled=True)
        return call_kernel(
            functools.partial(unpack_kernel, (tap_rows, tap_segs)),
            [shape((rows, width), BF16), shape(filter_taps.shape, F32)],
            (back,),
        )

    (sent,) = call_kernel(split_kernel, [shape((ctx, 2 * rows, own), BF16)], (grad_out, inputs))
    sent = lax.all_to_all(sent, "ctx", 0, 0, tiled=True)
    tap_parts = tap_parts.transpose(3, 2, 0, 1, 4).reshape(ctx * ch, tap_rows, tap_segs, own)
    tap_parts = lax.all_to_all(tap_parts, ("ctx", "ch"), 0, 0, tiled=True)
    tap_all = tap_parts.reshape(ctx, ch, tap_rows, tap_segs, own).transpose(1, 3, 0, 2, 4)
    input_grad, tap_grad = call_kernel(
        functools.partial(plain_kernel, block),
        [shape((ctx, rows, own), BF16), shape((taps, own), BF16)],
        (sent, tap_all.reshape(taps, own), forward, inverse),
        scratch,
        flops,
        (2, 3),
        sems=2,
    )
    back = lax.all_to_all(input_grad, "ctx", 0, 0, tiled=True)
    grad_inputs = back.transpose(1, 0, 2).reshape(rows, width)
    out_parts = tap_grad.reshape(ch, tap_segs, ctx, tap_rows, own).transpose(2, 0, 3, 1, 4)
    out_parts = out_parts.reshape(ctx * ch, tap_rows, tap_segs, own)
    out_parts = lax.all_to_all(out_parts, ("ctx", "ch"), 0, 0, tiled=True)
    out_parts = out_parts.reshape(ctx, ch, tap_rows, tap_segs, own).transpose(2, 3, 1, 0, 4)
    grad_taps = out_parts.reshape(tap_rows, tap_segs, channels).astype(F32)
    return grad_inputs, grad_taps


def solution(mesh):
    return jax.shard_map(
        shards,
        mesh=mesh,
        in_specs=(P("ctx", "ch"), P("ctx", "ch"), P("ctx", "ch", None)),
        out_specs=(P("ctx", "ch"), P("ctx", "ch", None)),
        check_vma=False,
    )
```

```python
import functools

import jax
import jax.numpy as jnp
import numpy as np
from jax import lax
from jax.experimental import pallas as pl
from jax.experimental.pallas import tpu as pltpu
from jax.sharding import PartitionSpec as P

F32 = jnp.float32
BF16 = jnp.bfloat16


def two_bf16(table):
    upper = table.astype(np.float32).astype(jnp.bfloat16)
    lower = (table - upper.astype(np.float64)).astype(np.float32).astype(jnp.bfloat16)
    return np.stack([upper, lower])


def dft_tables(block):
    freq = np.concatenate([np.arange(0, block, 2), np.arange(1, block, 2)])
    turns = ((2 * freq[:, None] + 1) * np.arange(block)[None, :]) % (4 * block)
    angle = turns * (np.pi / (2 * block))
    forward = np.concatenate([np.cos(angle), -np.sin(angle)], 0)
    return two_bf16(forward), two_bf16(forward.T / block)


def forward_dft(table, columns):
    first = jnp.dot(table[0], columns, preferred_element_type=F32)
    return first + jnp.dot(table[1], columns, preferred_element_type=F32)


def inverse_dft(table, spec):
    head = spec.astype(BF16)
    tail = (spec - head.astype(F32)).astype(BF16)
    total = jnp.dot(table[0], head, preferred_element_type=F32)
    total += jnp.dot(table[1], head, preferred_element_type=F32)
    return total + jnp.dot(table[0], tail, preferred_element_type=F32)


def side_by_side(width):
    return 2 if width % 128 == 0 else 1


def spectra(table, block, load, spec_ref):
    count, _, width = spec_ref.shape
    group = side_by_side(width)

    def step(j):
        parts = [load(j + u) for u in range(group)]
        both = forward_dft(table, jnp.concatenate(parts, 1) if group > 1 else parts[0])
        for u in range(group):
            spec_ref[j + u] = both[:, u * width : (u + 1) * width]

    return [functools.partial(step, j) for j in range(0, count, group)]


def correlate(block, left_ref, grad_ref, out_ref, beside=()):
    lefts, outs, count = left_ref.shape[0], out_ref.shape[0], grad_ref.shape[0]
    tiles = block // 8

    def pieces(ref, real, imag):
        return [(ref[j, real], ref[j, imag]) for j in range(ref.shape[0])]

    def tile(sign, real, imag):
        grad, left = pieces(grad_ref, real, imag), pieces(left_ref, real, imag)
        window = []
        for j in range(count):
            re, im = grad[j]
            if j + 1 < count:
                next_re, next_im = grad[j + 1]
                re, im = (re + next_im, im - next_re) if sign > 0 else (re - next_im, im + next_re)
            window.append((re, im))
        for a in range(outs):
            sum_real = sum_imag = None
            for (lr, li), (wr, wi) in zip(left, window[a:]):
                re, im = lr * wr + li * wi, lr * wi - li * wr
                sum_real = re if sum_real is None else sum_real + re
                sum_imag = im if sum_imag is None else sum_imag + im
            out_ref[a, real], out_ref[a, imag] = sum_real, sum_imag

    def body(sign, first, t, carry):
        at = pl.multiple_of(first + t * 8, 8)
        tile(sign, pl.ds(at, 8), pl.ds(pl.multiple_of(block + at, 8), 8))
        return carry

    if not beside:
        for sign, first in ((1, 0), (-1, block // 2)):
            lax.fori_loop(0, tiles // 2, functools.partial(body, sign, first), 0)
        return
    each = tiles // len(beside)
    for k, step in enumerate(beside):
        step()
        for t in range(k * each, (k + 1) * each):
            tile(1 if 2 * t < tiles else -1, pl.ds(t * 8, 8), pl.ds(block + t * 8, 8))


def invert(table, block, spec_ref, store):
    count, _, width = spec_ref.shape
    group = side_by_side(width)

    def step(j):
        parts = [spec_ref[j + u] for u in range(group)]
        both = inverse_dft(table, jnp.concatenate(parts, 1) if group > 1 else parts[0])
        for u in range(group):
            store(j + u, both[:, u * width : (u + 1) * width].astype(BF16))

    return [functools.partial(step, j) for j in range(0, count, group)]


def run(steps):
    for step in steps:
        step()


def fetch(pairs, sems):
    copies = [pltpu.make_async_copy(far, near, sems.at[k]) for k, (far, near) in enumerate(pairs)]
    for copy in copies:
        copy.start()
    return copies


def half_of(ref, rows, half):
    def load(j):
        return jnp.concatenate([ref[2 * j + u, pl.ds(half * rows, rows), :] for u in range(2)], 0)

    return load


def both_grads(block, loads, stores, refs):
    forward, inverse, fv, iv, grad_spec, value_spec, spec, tap_spec, tap_sum, sems = refs
    copies = fetch([(forward, fv), (inverse, iv)], sems)
    (ready_grad, load_grad), (ready_value, load_value), (ready_taps, load_taps) = loads
    ready_grad()
    copies[0].wait()
    copies[1].wait()
    ready_taps()
    run(spectra(fv, block, load_grad, grad_spec))
    ready_value()
    run(spectra(fv, block, load_taps, tap_spec))
    value_steps = spectra(fv, block, load_value, value_spec)
    grad_steps = invert(iv, block, spec, stores[0])
    if len(value_steps) > 8:
        run(value_steps)
        value_steps = ()
    correlate(block, tap_spec, grad_spec, spec, value_steps)
    if len(grad_steps) > 8:
        run(grad_steps)
        grad_steps = ()
    correlate(block, value_spec, grad_spec, tap_sum, grad_steps)
    run(invert(iv, block, tap_sum, stores[1]))


def plain_kernel(block, sent_ref, taps_ref, forward, inverse, grad_ref, tap_grad_ref, *refs):
    rows = block // 2

    loads = (
        (tuple, half_of(sent_ref, rows, 0)),
        (tuple, half_of(sent_ref, rows, 1)),
        (tuple, lambda j: taps_ref[pl.ds(j * block, block), :]),
    )

    def store_grad(j, result):
        for u in range(2):
            grad_ref[2 * j + u] = result[u * rows : (u + 1) * rows]

    def store_taps(j, result):
        tap_grad_ref[pl.ds(j * block, block), :] = result

    both_grads(block, loads, (store_grad, store_taps), (forward, inverse, *refs))


def traded(top, bottom):
    half = top.shape[1] // 2
    left = lax.broadcasted_iota(jnp.int32, top.shape, 1) < half
    return (
        jnp.where(left, top, pltpu.roll(bottom, half, 1)),
        jnp.where(left, pltpu.roll(top, half, 1), bottom),
    )


def pack_kernel(grad_ref, value_ref, taps_ref, out_ref):
    half = grad_ref.shape[0] // 2
    own, size = out_ref.shape[2], taps_ref.shape[2]
    for i in range(out_ref.shape[0] // 2):
        columns = pl.ds(i * own, own)
        for n, ref in enumerate((grad_ref, value_ref)):
            pair = traded(ref[pl.ds(0, half), columns].astype(F32), ref[pl.ds(half, half), columns].astype(F32))
            for j in range(2):
                out_ref[2 * i + j, pl.ds(n * half, half), :] = pair[j].astype(BF16)
        pair = traded(taps_ref[0, i].astype(F32), taps_ref[1, i].astype(F32))
        for j in range(2):
            out_ref[2 * i + j, pl.ds(2 * half, size), :] = pair[j].astype(BF16)


def paired_kernel(sizes, sent_ref, forward, inverse, out_ref, whole, taps, *refs):
    block, size, tap_segs = sizes
    rows, half = block // 2, block // 4
    count = sent_ref.shape[0] // 2

    def untrade(n):
        for i in range(count):
            pair = [sent_ref[2 * i + j, pl.ds(n * half, half), :].astype(F32) for j in range(2)]
            for u, part in enumerate(traded(*pair)):
                whole[n, pl.ds(i * rows + u * half, half), :] = part.astype(BF16)

    def gather_taps():
        for i in range(count):
            for j in range(2):
                taps[j, pl.ds(i * size, size), :] = sent_ref[2 * i + j, pl.ds(2 * half, size), :].astype(F32)

    loads = (
        (functools.partial(untrade, 0), lambda j: whole[0, pl.ds(j * block, block), :]),
        (functools.partial(untrade, 1), lambda j: whole[1, pl.ds(j * block, block), :]),
        (gather_taps, lambda j: jnp.concatenate([taps[segment(2 * j + u)].astype(BF16) for u in range(2)], 0)),
    )

    def segment(s):
        return s // tap_segs, pl.ds(s % tap_segs, rows, stride=tap_segs), slice(None)

    def store_grad(j, result):
        for u in range(2):
            at = u * rows
            result32 = result.astype(F32)
            pair = traded(result32[at : at + half], result32[at + half : at + rows])
            for side in range(2):
                out_ref[2 * (2 * j + u) + side, pl.ds(0, half), :] = pair[side].astype(BF16)

    def store_taps(j, result):
        for u in range(2):
            taps[segment(2 * j + u)] = result[u * rows : (u + 1) * rows].astype(F32)
        if (2 * j + 2) % tap_segs:
            return
        side = 2 * j // tap_segs
        for i in range(count):
            out_ref[2 * i + side, pl.ds(half, size), :] = taps[side, pl.ds(i * size, size), :].astype(BF16)

    both_grads(block, loads, (store_grad, store_taps), (forward, inverse, *refs))


def unpack_kernel(back_ref, grad_ref, taps_ref):
    rows, width = grad_ref.shape
    half, own = rows // 2, back_ref.shape[2]
    tap_rows, tap_segs = taps_ref.shape[:2]
    size = tap_rows * tap_segs
    for i in range(back_ref.shape[0] // 2):
        pair = traded(*[back_ref[2 * i + j, pl.ds(0, half), :].astype(F32) for j in range(2)])
        for u in range(2):
            grad_ref[pl.ds(u * half, half), pl.ds(i * own, own)] = pair[u].astype(BF16)
        pair = traded(*[back_ref[2 * i + j, pl.ds(half, size), :].astype(F32) for j in range(2)])
        for side in range(2):
            taps_ref[:, :, pl.ds(side * width + i * own, own)] = pair[side].reshape(tap_rows, tap_segs, own)


def split_kernel(*refs):
    ins, out_ref = refs[:-1], refs[-1]
    count, size, own = out_ref.shape
    rows = size // len(ins)
    for k in range(count):
        for n, ref in enumerate(ins):
            out_ref[k, pl.ds(n * rows, rows), :] = ref[:, k * own : (k + 1) * own]


def call_kernel(body, out_shape, operands, scratch=(), flops=0, far=(), sems=0):
    held = [a for k, a in enumerate(operands) if k not in far]
    held += list(out_shape) + list(scratch)
    padded = sum(int(np.prod(a.shape[:-1])) * max(a.shape[-1], 128) * a.dtype.itemsize for a in held)
    moved = sum(int(np.prod(a.shape)) * a.dtype.itemsize for a in list(operands) + list(out_shape))
    near, away = pl.BlockSpec(memory_space=pltpu.VMEM), pl.BlockSpec(memory_space=pl.ANY)
    scratch_shapes = [pltpu.VMEM(a.shape, a.dtype) for a in scratch]
    if sems:
        scratch_shapes.append(pltpu.SemaphoreType.DMA((sems,)))
    return pl.pallas_call(
        body,
        out_shape=out_shape,
        in_specs=[away if k in far else near for k in range(len(operands))],
        out_specs=[near] * len(out_shape),
        scratch_shapes=scratch_shapes,
        compiler_params=pltpu.CompilerParams(vmem_limit_bytes=min(padded + (6 << 20), 56 << 20)),
        cost_estimate=pl.CostEstimate(flops=flops, bytes_accessed=moved, transcendentals=0),
    )(*operands)


def shards(grad_out, inputs, filter_taps):
    rows, width = grad_out.shape
    ctx, ch = lax.axis_size("ctx"), lax.axis_size("ch")
    tap_rows, tap_segs, channels = filter_taps.shape
    own = width // ctx
    block = 2 * rows
    taps = rows * tap_segs * ch
    size = tap_rows * tap_segs
    blocks, tap_blocks = rows * ctx // block, taps // block
    shape = jax.ShapeDtypeStruct
    paired = own == 128 and ch == 2 and rows % 32 == 0 and size % 16 == 0 and tap_segs % 2 == 0

    forward, inverse = (jnp.asarray(t) for t in dft_tables(block))
    spec = shape((blocks, 2 * block, own), F32)
    tap_spec = shape((tap_blocks, 2 * block, own), F32)
    scratch = [shape(forward.shape, BF16), shape(inverse.shape, BF16), spec, spec, spec, tap_spec, tap_spec]
    flops = 4 * block * block * own * 5 * (blocks + tap_blocks)
    tap_parts = filter_taps.reshape(tap_rows, tap_segs, ch, ctx, own)

    if paired:
        tap_parts = tap_parts.transpose(2, 3, 0, 1, 4).reshape(ch, ctx, size, own)
        (sent,) = call_kernel(
            pack_kernel, [shape((ctx * ch, rows + size, own), BF16)], (grad_out, inputs, tap_parts)
        )
        sent = lax.all_to_all(sent, ("ctx", "ch"), 0, 0, tiled=True)
        (back,) = call_kernel(
            functools.partial(paired_kernel, (block, size, tap_segs)),
            [shape((ctx * ch, rows // 2 + size, own), BF16)],
            (sent, forward, inverse),
            [shape((2, rows * ctx, own), BF16), shape((ch, rows * tap_segs, own), F32)] + scratch,
            flops,
            (1, 2),
            sems=2,
        )
        back = lax.all_to_all(back, ("ctx", "ch"), 0, 0, tiled=True)
        return call_kernel(
            unpack_kernel,
            [shape((rows, width), BF16), shape(filter_taps.shape, F32)],
            (back,),
        )

    (sent,) = call_kernel(split_kernel, [shape((ctx, 2 * rows, own), BF16)], (grad_out, inputs))
    sent = lax.all_to_all(sent, "ctx", 0, 0, tiled=True)
    tap_parts = tap_parts.transpose(3, 2, 0, 1, 4).reshape(ctx * ch, tap_rows, tap_segs, own)
    tap_parts = lax.all_to_all(tap_parts, ("ctx", "ch"), 0, 0, tiled=True)
    tap_all = tap_parts.reshape(ctx, ch, tap_rows, tap_segs, own).transpose(1, 3, 0, 2, 4)
    input_grad, tap_grad = call_kernel(
        functools.partial(plain_kernel, block),
        [shape((ctx, rows, own), BF16), shape((taps, own), BF16)],
        (sent, tap_all.reshape(taps, own), forward, inverse),
        scratch,
        flops,
        (2, 3),
        sems=2,
    )
    back = lax.all_to_all(input_grad, "ctx", 0, 0, tiled=True)
    grad_inputs = back.transpose(1, 0, 2).reshape(rows, width)
    out_parts = tap_grad.reshape(ch, tap_segs, ctx, tap_rows, own).transpose(2, 0, 3, 1, 4)
    out_parts = out_parts.reshape(ctx * ch, tap_rows, tap_segs, own)
    out_parts = lax.all_to_all(out_parts, ("ctx", "ch"), 0, 0, tiled=True)
    out_parts = out_parts.reshape(ctx, ch, tap_rows, tap_segs, own).transpose(2, 3, 1, 0, 4)
    grad_taps = out_parts.reshape(tap_rows, tap_segs, channels).astype(F32)
    return grad_inputs, grad_taps


def solution(mesh):
    return jax.shard_map(
        shards,
        mesh=mesh,
        in_specs=(P("ctx", "ch"), P("ctx", "ch"), P("ctx", "ch", None)),
        out_specs=(P("ctx", "ch"), P("ctx", "ch", None)),
        check_vma=False,
    )
```

```python
import functools

import jax
import jax.numpy as jnp
import numpy as np
from jax import lax
from jax.experimental import pallas as pl
from jax.experimental.pallas import tpu as pltpu
from jax.sharding import PartitionSpec as P

F32 = jnp.float32
BF16 = jnp.bfloat16


def two_bf16(table):
    upper = table.astype(np.float32).astype(jnp.bfloat16)
    lower = (table - upper.astype(np.float64)).astype(np.float32).astype(jnp.bfloat16)
    return np.stack([upper, lower])


def dft_tables(block):
    freq = np.concatenate([np.arange(0, block, 2), np.arange(1, block, 2)])
    turns = ((2 * freq[:, None] + 1) * np.arange(block)[None, :]) % (4 * block)
    angle = turns * (np.pi / (2 * block))
    forward = np.concatenate([np.cos(angle), -np.sin(angle)], 0)
    return two_bf16(forward), two_bf16(forward.T / block)


def forward_dft(table, columns):
    first = jnp.dot(table[0], columns, preferred_element_type=F32)
    return first + jnp.dot(table[1], columns, preferred_element_type=F32)


def inverse_dft(table, spec):
    spec = spec.astype(BF16)
    first = jnp.dot(table[0], spec, preferred_element_type=F32)
    return first + jnp.dot(table[1], spec, preferred_element_type=F32)


def side_by_side(width):
    return 2 if width % 128 == 0 else 1


def spectra(table, block, load, spec_ref):
    count, _, width = spec_ref.shape
    group = side_by_side(width)

    def step(j):
        parts = [load(j + u) for u in range(group)]
        both = forward_dft(table, jnp.concatenate(parts, 1) if group > 1 else parts[0])
        for u in range(group):
            spec_ref[j + u] = both[:, u * width : (u + 1) * width]

    return [functools.partial(step, j) for j in range(0, count, group)]


def correlate(block, left_ref, grad_ref, out_ref, beside=()):
    lefts, outs, count = left_ref.shape[0], out_ref.shape[0], grad_ref.shape[0]
    tiles = block // 8

    def pieces(ref, real, imag):
        return [(ref[j, real], ref[j, imag]) for j in range(ref.shape[0])]

    def tile(sign, real, imag):
        grad, left = pieces(grad_ref, real, imag), pieces(left_ref, real, imag)
        window = []
        for j in range(count):
            re, im = grad[j]
            if j + 1 < count:
                next_re, next_im = grad[j + 1]
                re, im = (re + next_im, im - next_re) if sign > 0 else (re - next_im, im + next_re)
            window.append((re, im, re + im))
        left = [(re, im, re - im) for re, im in left]
        for a in range(outs):
            terms = [[l * w for l, w in zip(*pair)] for pair in zip(left, window[a:])]
            reals, imags, mixed = (functools.reduce(lambda x, y: x + y, column) for column in zip(*terms))
            out_ref[a, real], out_ref[a, imag] = reals + imags, mixed - (reals - imags)

    def body(sign, first, t, carry):
        at = pl.multiple_of(first + t * 8, 8)
        tile(sign, pl.ds(at, 8), pl.ds(pl.multiple_of(block + at, 8), 8))
        return carry

    if not beside:
        for sign, first in ((1, 0), (-1, block // 2)):
            lax.fori_loop(0, tiles // 2, functools.partial(body, sign, first), 0)
        return
    each = tiles // len(beside)
    for k, step in enumerate(beside):
        step()
        for t in range(k * each, (k + 1) * each):
            tile(1 if 2 * t < tiles else -1, pl.ds(t * 8, 8), pl.ds(block + t * 8, 8))


def invert(table, block, spec_ref, store):
    count, _, width = spec_ref.shape
    group = side_by_side(width)

    def step(j):
        parts = [spec_ref[j + u] for u in range(group)]
        both = inverse_dft(table, jnp.concatenate(parts, 1) if group > 1 else parts[0])
        for u in range(group):
            store(j + u, both[:, u * width : (u + 1) * width].astype(BF16))

    return [functools.partial(step, j) for j in range(0, count, group)]


def run(steps):
    for step in steps:
        step()


def half_of(ref, rows, half):
    def load(j):
        return jnp.concatenate([ref[2 * j + u, pl.ds(half * rows, rows), :] for u in range(2)], 0)

    return load


def both_grads(block, loads, stores, refs):
    forward, inverse, grad_spec, value_spec, spec, tap_spec, tap_sum = refs
    (ready_grad, load_grad), (ready_value, load_value), (ready_taps, load_taps) = loads
    ready_grad()
    ready_taps()
    run(spectra(forward, block, load_grad, grad_spec))
    ready_value()
    run(spectra(forward, block, load_taps, tap_spec))
    value_steps = spectra(forward, block, load_value, value_spec)
    grad_steps = invert(inverse, block, spec, stores[0])
    if len(value_steps) > 8:
        run(value_steps)
        value_steps = ()
    correlate(block, tap_spec, grad_spec, spec, value_steps)
    if len(grad_steps) > 8:
        run(grad_steps)
        grad_steps = ()
    correlate(block, value_spec, grad_spec, tap_sum, grad_steps)
    run(invert(inverse, block, tap_sum, stores[1]))


def plain_kernel(block, sent_ref, taps_ref, forward, inverse, grad_ref, tap_grad_ref, *refs):
    rows = block // 2

    loads = (
        (tuple, half_of(sent_ref, rows, 0)),
        (tuple, half_of(sent_ref, rows, 1)),
        (tuple, lambda j: taps_ref[pl.ds(j * block, block), :]),
    )

    def store_grad(j, result):
        for u in range(2):
            grad_ref[2 * j + u] = result[u * rows : (u + 1) * rows]

    def store_taps(j, result):
        tap_grad_ref[pl.ds(j * block, block), :] = result

    both_grads(block, loads, (store_grad, store_taps), (forward, inverse, *refs))


def traded(top, bottom):
    half = top.shape[1] // 2
    left = lax.broadcasted_iota(jnp.int32, top.shape, 1) < half
    return (
        jnp.where(left, top, pltpu.roll(bottom, half, 1)),
        jnp.where(left, pltpu.roll(top, half, 1), bottom),
    )


def pack_kernel(grad_ref, value_ref, taps_ref, out_ref):
    half = grad_ref.shape[0] // 2
    own, size = out_ref.shape[2], taps_ref.shape[2]
    for i in range(out_ref.shape[0] // 2):
        columns = pl.ds(i * own, own)
        for n, ref in enumerate((grad_ref, value_ref)):
            pair = traded(ref[pl.ds(0, half), columns].astype(F32), ref[pl.ds(half, half), columns].astype(F32))
            for j in range(2):
                out_ref[2 * i + j, pl.ds(n * half, half), :] = pair[j].astype(BF16)
        pair = traded(taps_ref[0, i].astype(F32), taps_ref[1, i].astype(F32))
        for j in range(2):
            out_ref[2 * i + j, pl.ds(2 * half, size), :] = pair[j].astype(BF16)


def paired_kernel(sizes, sent_ref, forward, inverse, out_ref, whole, taps, *refs):
    block, size, tap_segs = sizes
    rows, half = block // 2, block // 4
    count = sent_ref.shape[0] // 2

    def untrade(n):
        for i in range(count):
            pair = [sent_ref[2 * i + j, pl.ds(n * half, half), :].astype(F32) for j in range(2)]
            for u, part in enumerate(traded(*pair)):
                whole[n, pl.ds(i * rows + u * half, half), :] = part.astype(BF16)

    def gather_taps():
        for i in range(count):
            for j in range(2):
                taps[j, pl.ds(i * size, size), :] = sent_ref[2 * i + j, pl.ds(2 * half, size), :].astype(F32)

    loads = (
        (functools.partial(untrade, 0), lambda j: whole[0, pl.ds(j * block, block), :]),
        (functools.partial(untrade, 1), lambda j: whole[1, pl.ds(j * block, block), :]),
        (gather_taps, lambda j: jnp.concatenate([taps[segment(2 * j + u)].astype(BF16) for u in range(2)], 0)),
    )

    def segment(s):
        return s // tap_segs, pl.ds(s % tap_segs, rows, stride=tap_segs), slice(None)

    def store_grad(j, result):
        for u in range(2):
            at = u * rows
            result32 = result.astype(F32)
            pair = traded(result32[at : at + half], result32[at + half : at + rows])
            for side in range(2):
                out_ref[2 * (2 * j + u) + side, pl.ds(0, half), :] = pair[side].astype(BF16)

    def store_taps(j, result):
        for u in range(2):
            taps[segment(2 * j + u)] = result[u * rows : (u + 1) * rows].astype(F32)
        if (2 * j + 2) % tap_segs:
            return
        side = 2 * j // tap_segs
        for i in range(count):
            out_ref[2 * i + side, pl.ds(half, size), :] = taps[side, pl.ds(i * size, size), :].astype(BF16)

    both_grads(block, loads, (store_grad, store_taps), (forward, inverse, *refs))


def unpack_kernel(back_ref, grad_ref, taps_ref):
    rows, width = grad_ref.shape
    half, own = rows // 2, back_ref.shape[2]
    tap_rows, tap_segs = taps_ref.shape[:2]
    size = tap_rows * tap_segs
    for i in range(back_ref.shape[0] // 2):
        pair = traded(*[back_ref[2 * i + j, pl.ds(0, half), :].astype(F32) for j in range(2)])
        for u in range(2):
            grad_ref[pl.ds(u * half, half), pl.ds(i * own, own)] = pair[u].astype(BF16)
        pair = traded(*[back_ref[2 * i + j, pl.ds(half, size), :].astype(F32) for j in range(2)])
        for side in range(2):
            taps_ref[:, :, pl.ds(side * width + i * own, own)] = pair[side].reshape(tap_rows, tap_segs, own)


def split_kernel(*refs):
    ins, out_ref = refs[:-1], refs[-1]
    count, size, own = out_ref.shape
    rows = size // len(ins)
    for k in range(count):
        for n, ref in enumerate(ins):
            out_ref[k, pl.ds(n * rows, rows), :] = ref[:, k * own : (k + 1) * own]


def call_kernel(body, out_shape, operands, scratch=(), flops=0, far=(), sems=0):
    held = [a for k, a in enumerate(operands) if k not in far]
    held += list(out_shape) + list(scratch)
    padded = sum(int(np.prod(a.shape[:-1])) * max(a.shape[-1], 128) * a.dtype.itemsize for a in held)
    moved = sum(int(np.prod(a.shape)) * a.dtype.itemsize for a in list(operands) + list(out_shape))
    near, away = pl.BlockSpec(memory_space=pltpu.VMEM), pl.BlockSpec(memory_space=pl.ANY)
    scratch_shapes = [pltpu.VMEM(a.shape, a.dtype) for a in scratch]
    if sems:
        scratch_shapes.append(pltpu.SemaphoreType.DMA((sems,)))
    return pl.pallas_call(
        body,
        out_shape=out_shape,
        in_specs=[away if k in far else near for k in range(len(operands))],
        out_specs=[near] * len(out_shape),
        scratch_shapes=scratch_shapes,
        compiler_params=pltpu.CompilerParams(vmem_limit_bytes=min(padded + (6 << 20), 56 << 20)),
        cost_estimate=pl.CostEstimate(flops=flops, bytes_accessed=moved, transcendentals=0),
    )(*operands)


def shards(grad_out, inputs, filter_taps):
    rows, width = grad_out.shape
    ctx, ch = lax.axis_size("ctx"), lax.axis_size("ch")
    tap_rows, tap_segs, channels = filter_taps.shape
    own = width // ctx
    block = 2 * rows
    taps = rows * tap_segs * ch
    size = tap_rows * tap_segs
    blocks, tap_blocks = rows * ctx // block, taps // block
    shape = jax.ShapeDtypeStruct
    paired = own == 128 and ch == 2 and rows % 32 == 0 and size % 16 == 0 and tap_segs % 2 == 0

    forward, inverse = (jnp.asarray(t) for t in dft_tables(block))
    spec = shape((blocks, 2 * block, own), F32)
    tap_spec = shape((tap_blocks, 2 * block, own), F32)
    scratch = [spec, spec, spec, tap_spec, tap_spec]
    flops = 4 * block * block * own * 5 * (blocks + tap_blocks)
    tap_parts = filter_taps.reshape(tap_rows, tap_segs, ch, ctx, own)

    if paired:
        tap_parts = tap_parts.transpose(2, 3, 0, 1, 4).reshape(ch, ctx, size, own)
        (sent,) = call_kernel(
            pack_kernel, [shape((ctx * ch, rows + size, own), BF16)], (grad_out, inputs, tap_parts)
        )
        sent = lax.all_to_all(sent, ("ctx", "ch"), 0, 0, tiled=True)
        (back,) = call_kernel(
            functools.partial(paired_kernel, (block, size, tap_segs)),
            [shape((ctx * ch, rows // 2 + size, own), BF16)],
            (sent, forward, inverse),
            [shape((2, rows * ctx, own), BF16), shape((ch, rows * tap_segs, own), F32)] + scratch,
            flops,
        )
        back = lax.all_to_all(back, ("ctx", "ch"), 0, 0, tiled=True)
        return call_kernel(
            unpack_kernel,
            [shape((rows, width), BF16), shape(filter_taps.shape, F32)],
            (back,),
        )

    (sent,) = call_kernel(split_kernel, [shape((ctx, 2 * rows, own), BF16)], (grad_out, inputs))
    sent = lax.all_to_all(sent, "ctx", 0, 0, tiled=True)
    tap_parts = tap_parts.transpose(3, 2, 0, 1, 4).reshape(ctx * ch, tap_rows, tap_segs, own)
    tap_parts = lax.all_to_all(tap_parts, ("ctx", "ch"), 0, 0, tiled=True)
    tap_all = tap_parts.reshape(ctx, ch, tap_rows, tap_segs, own).transpose(1, 3, 0, 2, 4)
    input_grad, tap_grad = call_kernel(
        functools.partial(plain_kernel, block),
        [shape((ctx, rows, own), BF16), shape((taps, own), BF16)],
        (sent, tap_all.reshape(taps, own), forward, inverse),
        scratch,
        flops,
    )
    back = lax.all_to_all(input_grad, "ctx", 0, 0, tiled=True)
    grad_inputs = back.transpose(1, 0, 2).reshape(rows, width)
    out_parts = tap_grad.reshape(ch, tap_segs, ctx, tap_rows, own).transpose(2, 0, 3, 1, 4)
    out_parts = out_parts.reshape(ctx * ch, tap_rows, tap_segs, own)
    out_parts = lax.all_to_all(out_parts, ("ctx", "ch"), 0, 0, tiled=True)
    out_parts = out_parts.reshape(ctx, ch, tap_rows, tap_segs, own).transpose(2, 3, 1, 0, 4)
    grad_taps = out_parts.reshape(tap_rows, tap_segs, channels).astype(F32)
    return grad_inputs, grad_taps


def solution(mesh):
    return jax.shard_map(
        shards,
        mesh=mesh,
        in_specs=(P("ctx", "ch"), P("ctx", "ch"), P("ctx", "ch", None)),
        out_specs=(P("ctx", "ch"), P("ctx", "ch", None)),
        check_vma=False,
    )
```

```python
import functools

import jax
import jax.numpy as jnp
import numpy as np
from jax import lax
from jax.experimental import pallas as pl
from jax.experimental.pallas import tpu as pltpu
from jax.sharding import PartitionSpec as P

F32 = jnp.float32
BF16 = jnp.bfloat16


def two_bf16(table):
    upper = table.astype(np.float32).astype(jnp.bfloat16)
    lower = (table - upper.astype(np.float64)).astype(np.float32).astype(jnp.bfloat16)
    return np.stack([upper, lower])


def dft_tables(block):
    freq = np.concatenate([np.arange(0, block, 2), np.arange(1, block, 2)])
    turns = ((2 * freq[:, None] + 1) * np.arange(block)[None, :]) % (4 * block)
    angle = turns * (np.pi / (2 * block))
    forward = np.concatenate([np.cos(angle), -np.sin(angle)], 0)
    return two_bf16(forward), two_bf16(forward.T / block)


def forward_dft(table, columns):
    first = jnp.dot(table[0], columns, preferred_element_type=F32)
    return first + jnp.dot(table[1], columns, preferred_element_type=F32)


def inverse_dft(table, spec):
    spec = spec.astype(BF16)
    first = jnp.dot(table[0], spec, preferred_element_type=F32)
    return first + jnp.dot(table[1], spec, preferred_element_type=F32)


def side_by_side(width):
    return 2 if width % 128 == 0 else 1


def spectra(table, block, load, spec_ref):
    count, _, width = spec_ref.shape
    group = side_by_side(width)

    def step(j):
        parts = [load(j + u) for u in range(group)]
        both = forward_dft(table, jnp.concatenate(parts, 1) if group > 1 else parts[0])
        for u in range(group):
            spec_ref[j + u] = both[:, u * width : (u + 1) * width]

    return [functools.partial(step, j) for j in range(0, count, group)]


def correlate(block, left_ref, grad_ref, out_ref, beside=()):
    lefts, outs, count = left_ref.shape[0], out_ref.shape[0], grad_ref.shape[0]
    tiles = block // 8

    def pieces(ref, real, imag):
        return [(ref[j, real], ref[j, imag]) for j in range(ref.shape[0])]

    def tile(sign, real, imag):
        grad, left = pieces(grad_ref, real, imag), pieces(left_ref, real, imag)
        window = []
        for j in range(count):
            re, im = grad[j]
            if j + 1 < count:
                next_re, next_im = grad[j + 1]
                re, im = (re + next_im, im - next_re) if sign > 0 else (re - next_im, im + next_re)
            window.append((re, im, re + im))
        left = [(re, im, re - im) for re, im in left]
        for a in range(outs):
            terms = [[l * w for l, w in zip(*pair)] for pair in zip(left, window[a:])]
            reals, imags, mixed = (functools.reduce(lambda x, y: x + y, column) for column in zip(*terms))
            out_ref[a, real], out_ref[a, imag] = reals + imags, mixed - (reals - imags)

    def body(sign, first, t, carry):
        at = pl.multiple_of(first + t * 8, 8)
        tile(sign, pl.ds(at, 8), pl.ds(pl.multiple_of(block + at, 8), 8))
        return carry

    if not beside:
        for sign, first in ((1, 0), (-1, block // 2)):
            lax.fori_loop(0, tiles // 2, functools.partial(body, sign, first), 0)
        return
    each = tiles // len(beside)
    for k, step in enumerate(beside):
        step()
        for t in range(k * each, (k + 1) * each):
            tile(1 if 2 * t < tiles else -1, pl.ds(t * 8, 8), pl.ds(block + t * 8, 8))


def invert(table, block, spec_ref, store):
    count, _, width = spec_ref.shape
    group = side_by_side(width)

    def step(j):
        parts = [spec_ref[j + u] for u in range(group)]
        both = inverse_dft(table, jnp.concatenate(parts, 1) if group > 1 else parts[0])
        for u in range(group):
            store(j + u, both[:, u * width : (u + 1) * width])

    return [functools.partial(step, j) for j in range(0, count, group)]


def run(steps):
    for step in steps:
        step()


def half_of(ref, rows, half):
    def load(j):
        return jnp.concatenate([ref[2 * j + u, pl.ds(half * rows, rows), :] for u in range(2)], 0)

    return load


def both_grads(block, loads, stores, refs):
    forward, inverse, grad_spec, value_spec, spec, tap_spec, tap_sum = refs
    (ready_grad, load_grad), (ready_value, load_value), (ready_taps, load_taps) = loads
    ready_grad()
    ready_taps()
    run(spectra(forward, block, load_grad, grad_spec))
    ready_value()
    run(spectra(forward, block, load_taps, tap_spec))
    value_steps = spectra(forward, block, load_value, value_spec)
    grad_steps = invert(inverse, block, spec, stores[0])
    if len(value_steps) > 8:
        run(value_steps)
        value_steps = ()
    correlate(block, tap_spec, grad_spec, spec, value_steps)
    if len(grad_steps) > 8:
        run(grad_steps)
        grad_steps = ()
    correlate(block, value_spec, grad_spec, tap_sum, grad_steps)
    run(invert(inverse, block, tap_sum, stores[1]))


def plain_kernel(block, sent_ref, taps_ref, forward, inverse, grad_ref, tap_grad_ref, *refs):
    rows = block // 2

    loads = (
        (tuple, half_of(sent_ref, rows, 0)),
        (tuple, half_of(sent_ref, rows, 1)),
        (tuple, lambda j: taps_ref[pl.ds(j * block, block), :]),
    )

    def store_grad(j, result):
        for u in range(2):
            grad_ref[2 * j + u] = result[u * rows : (u + 1) * rows].astype(BF16)

    def store_taps(j, result):
        tap_grad_ref[pl.ds(j * block, block), :] = result.astype(BF16)

    both_grads(block, loads, (store_grad, store_taps), (forward, inverse, *refs))


def traded(top, bottom):
    half = top.shape[1] // 2
    left = lax.broadcasted_iota(jnp.int32, top.shape, 1) < half
    return (
        jnp.where(left, top, pltpu.roll(bottom, half, 1)),
        jnp.where(left, pltpu.roll(top, half, 1), bottom),
    )


def pack_kernel(grad_ref, value_ref, taps_ref, out_ref):
    half = grad_ref.shape[0] // 2
    own, size = out_ref.shape[2], taps_ref.shape[2]
    for i in range(out_ref.shape[0] // 2):
        columns = pl.ds(i * own, own)
        for n, ref in enumerate((grad_ref, value_ref)):
            pair = traded(ref[pl.ds(0, half), columns], ref[pl.ds(half, half), columns])
            for j in range(2):
                out_ref[2 * i + j, pl.ds(n * half, half), :] = pair[j]
        pair = traded(taps_ref[0, i], taps_ref[1, i])
        for j in range(2):
            out_ref[2 * i + j, pl.ds(2 * half, size), :] = pair[j]


def paired_kernel(sizes, sent_ref, forward, inverse, out_ref, whole, taps, *refs):
    block, size, tap_segs = sizes
    rows, half = block // 2, block // 4
    count = sent_ref.shape[0] // 2

    def untrade(n):
        for i in range(count):
            pair = [sent_ref[2 * i + j, pl.ds(n * half, half), :] for j in range(2)]
            for u, part in enumerate(traded(*pair)):
                whole[n, pl.ds(i * rows + u * half, half), :] = part

    def gather_taps():
        for i in range(count):
            for j in range(2):
                taps[j, pl.ds(i * size, size), :] = sent_ref[2 * i + j, pl.ds(2 * half, size), :].astype(F32)

    loads = (
        (functools.partial(untrade, 0), lambda j: whole[0, pl.ds(j * block, block), :]),
        (functools.partial(untrade, 1), lambda j: whole[1, pl.ds(j * block, block), :]),
        (gather_taps, lambda j: jnp.concatenate([taps[segment(2 * j + u)].astype(BF16) for u in range(2)], 0)),
    )

    def segment(s):
        return s // tap_segs, pl.ds(s % tap_segs, rows, stride=tap_segs), slice(None)

    def store_grad(j, result):
        result = result.astype(BF16)
        for u in range(2):
            at = u * rows
            pair = traded(result[at : at + half], result[at + half : at + rows])
            for side in range(2):
                out_ref[2 * (2 * j + u) + side, pl.ds(0, half), :] = pair[side]

    def store_taps(j, result):
        for u in range(2):
            taps[segment(2 * j + u)] = result[u * rows : (u + 1) * rows]
        if (2 * j + 2) % tap_segs:
            return
        side = 2 * j // tap_segs
        for i in range(count):
            out_ref[2 * i + side, pl.ds(half, size), :] = taps[side, pl.ds(i * size, size), :].astype(BF16)

    both_grads(block, loads, (store_grad, store_taps), (forward, inverse, *refs))


def unpack_kernel(back_ref, grad_ref, taps_ref):
    rows, width = grad_ref.shape
    half, own = rows // 2, back_ref.shape[2]
    tap_rows, tap_segs = taps_ref.shape[:2]
    size = tap_rows * tap_segs
    for i in range(back_ref.shape[0] // 2):
        pair = traded(*[back_ref[2 * i + j, pl.ds(0, half), :] for j in range(2)])
        for u in range(2):
            grad_ref[pl.ds(u * half, half), pl.ds(i * own, own)] = pair[u]
        pair = traded(*[back_ref[2 * i + j, pl.ds(half, size), :] for j in range(2)])
        for side in range(2):
            taps_ref[:, :, pl.ds(side * width + i * own, own)] = pair[side].astype(F32).reshape(tap_rows, tap_segs, own)


def split_kernel(*refs):
    ins, out_ref = refs[:-1], refs[-1]
    count, size, own = out_ref.shape
    rows = size // len(ins)
    for k in range(count):
        for n, ref in enumerate(ins):
            out_ref[k, pl.ds(n * rows, rows), :] = ref[:, k * own : (k + 1) * own]


def call_kernel(body, out_shape, operands, scratch=(), flops=0, far=(), sems=0):
    held = [a for k, a in enumerate(operands) if k not in far]
    held += list(out_shape) + list(scratch)
    padded = sum(int(np.prod(a.shape[:-1])) * max(a.shape[-1], 128) * a.dtype.itemsize for a in held)
    moved = sum(int(np.prod(a.shape)) * a.dtype.itemsize for a in list(operands) + list(out_shape))
    near, away = pl.BlockSpec(memory_space=pltpu.VMEM), pl.BlockSpec(memory_space=pl.ANY)
    scratch_shapes = [pltpu.VMEM(a.shape, a.dtype) for a in scratch]
    if sems:
        scratch_shapes.append(pltpu.SemaphoreType.DMA((sems,)))
    return pl.pallas_call(
        body,
        out_shape=out_shape,
        in_specs=[away if k in far else near for k in range(len(operands))],
        out_specs=[near] * len(out_shape),
        scratch_shapes=scratch_shapes,
        compiler_params=pltpu.CompilerParams(vmem_limit_bytes=min(padded + (6 << 20), 56 << 20)),
        cost_estimate=pl.CostEstimate(flops=flops, bytes_accessed=moved, transcendentals=0),
    )(*operands)


def shards(grad_out, inputs, filter_taps):
    rows, width = grad_out.shape
    ctx, ch = lax.axis_size("ctx"), lax.axis_size("ch")
    tap_rows, tap_segs, channels = filter_taps.shape
    own = width // ctx
    block = 2 * rows
    taps = rows * tap_segs * ch
    size = tap_rows * tap_segs
    blocks, tap_blocks = rows * ctx // block, taps // block
    shape = jax.ShapeDtypeStruct
    paired = own == 128 and ch == 2 and rows % 32 == 0 and size % 16 == 0 and tap_segs % 2 == 0

    forward, inverse = (jnp.asarray(t) for t in dft_tables(block))
    spec = shape((blocks, 2 * block, own), F32)
    tap_spec = shape((tap_blocks, 2 * block, own), F32)
    scratch = [spec, spec, spec, tap_spec, tap_spec]
    flops = 4 * block * block * own * 5 * (blocks + tap_blocks)
    tap_parts = filter_taps.reshape(tap_rows, tap_segs, ch, ctx, own)

    if paired:
        tap_parts = tap_parts.transpose(2, 3, 0, 1, 4).reshape(ch, ctx, size, own)
        (sent,) = call_kernel(
            pack_kernel, [shape((ctx * ch, rows + size, own), BF16)], (grad_out, inputs, tap_parts)
        )
        sent = lax.all_to_all(sent, ("ctx", "ch"), 0, 0, tiled=True)
        (back,) = call_kernel(
            functools.partial(paired_kernel, (block, size, tap_segs)),
            [shape((ctx * ch, rows // 2 + size, own), BF16)],
            (sent, forward, inverse),
            [shape((2, rows * ctx, own), BF16), shape((ch, rows * tap_segs, own), F32)] + scratch,
            flops,
        )
        back = lax.all_to_all(back, ("ctx", "ch"), 0, 0, tiled=True)
        return call_kernel(
            unpack_kernel,
            [shape((rows, width), BF16), shape(filter_taps.shape, F32)],
            (back,),
        )

    (sent,) = call_kernel(split_kernel, [shape((ctx, 2 * rows, own), BF16)], (grad_out, inputs))
    sent = lax.all_to_all(sent, "ctx", 0, 0, tiled=True)
    tap_parts = tap_parts.transpose(3, 2, 0, 1, 4).reshape(ctx * ch, tap_rows, tap_segs, own)
    tap_parts = lax.all_to_all(tap_parts, ("ctx", "ch"), 0, 0, tiled=True)
    tap_all = tap_parts.reshape(ctx, ch, tap_rows, tap_segs, own).transpose(1, 3, 0, 2, 4)
    input_grad, tap_grad = call_kernel(
        functools.partial(plain_kernel, block),
        [shape((ctx, rows, own), BF16), shape((taps, own), BF16)],
        (sent, tap_all.reshape(taps, own), forward, inverse),
        scratch,
        flops,
    )
    back = lax.all_to_all(input_grad, "ctx", 0, 0, tiled=True)
    grad_inputs = back.transpose(1, 0, 2).reshape(rows, width)
    out_parts = tap_grad.reshape(ch, tap_segs, ctx, tap_rows, own).transpose(2, 0, 3, 1, 4)
    out_parts = out_parts.reshape(ctx * ch, tap_rows, tap_segs, own)
    out_parts = lax.all_to_all(out_parts, ("ctx", "ch"), 0, 0, tiled=True)
    out_parts = out_parts.reshape(ctx, ch, tap_rows, tap_segs, own).transpose(2, 3, 1, 0, 4)
    grad_taps = out_parts.reshape(tap_rows, tap_segs, channels).astype(F32)
    return grad_inputs, grad_taps


def solution(mesh):
    return jax.shard_map(
        shards,
        mesh=mesh,
        in_specs=(P("ctx", "ch"), P("ctx", "ch"), P("ctx", "ch", None)),
        out_specs=(P("ctx", "ch"), P("ctx", "ch", None)),
        check_vma=False,
    )
```

```python
import functools

import jax
import jax.numpy as jnp
import numpy as np
from jax import lax
from jax.experimental import pallas as pl
from jax.experimental.pallas import tpu as pltpu
from jax.sharding import PartitionSpec as P

F32 = jnp.float32
BF16 = jnp.bfloat16


def two_bf16(table):
    upper = table.astype(np.float32).astype(jnp.bfloat16)
    lower = (table - upper.astype(np.float64)).astype(np.float32).astype(jnp.bfloat16)
    return np.stack([upper, lower])


def dft_tables(block):
    freq = np.concatenate([np.arange(0, block, 2), np.arange(1, block, 2)])
    turns = ((2 * freq[:, None] + 1) * np.arange(block)[None, :]) % (4 * block)
    angle = turns * (np.pi / (2 * block))
    forward = np.concatenate([np.cos(angle), -np.sin(angle)], 0)
    return two_bf16(forward), (forward.T / block).astype(np.float32).astype(jnp.bfloat16)


def forward_dft(table, columns):
    first = jnp.dot(table[0], columns, preferred_element_type=F32)
    return first + jnp.dot(table[1], columns, preferred_element_type=F32)


def inverse_dft(table, spec):
    return jnp.dot(table[...], spec.astype(BF16), preferred_element_type=F32)


def side_by_side(width):
    return 2 if width % 128 == 0 else 1


def spectra(table, block, load, spec_ref):
    count, _, width = spec_ref.shape
    group = side_by_side(width)

    def step(j):
        parts = [load(j + u) for u in range(group)]
        both = forward_dft(table, jnp.concatenate(parts, 1) if group > 1 else parts[0])
        for u in range(group):
            spec_ref[j + u] = both[:, u * width : (u + 1) * width]

    return [functools.partial(step, j) for j in range(0, count, group)]


def correlate(block, left_ref, grad_ref, out_ref, beside=()):
    lefts, outs, count = left_ref.shape[0], out_ref.shape[0], grad_ref.shape[0]
    tiles = block // 8

    def pieces(ref, real, imag):
        return [(ref[j, real], ref[j, imag]) for j in range(ref.shape[0])]

    def tile(sign, real, imag):
        grad, left = pieces(grad_ref, real, imag), pieces(left_ref, real, imag)
        window = []
        for j in range(count):
            re, im = grad[j]
            if j + 1 < count:
                next_re, next_im = grad[j + 1]
                re, im = (re + next_im, im - next_re) if sign > 0 else (re - next_im, im + next_re)
            window.append((re, im, re + im))
        left = [(re, im, re - im) for re, im in left]
        for a in range(outs):
            terms = [[l * w for l, w in zip(*pair)] for pair in zip(left, window[a:])]
            reals, imags, mixed = (functools.reduce(lambda x, y: x + y, column) for column in zip(*terms))
            out_ref[a, real], out_ref[a, imag] = reals + imags, mixed - (reals - imags)

    def body(sign, first, t, carry):
        at = pl.multiple_of(first + t * 8, 8)
        tile(sign, pl.ds(at, 8), pl.ds(pl.multiple_of(block + at, 8), 8))
        return carry

    if not beside:
        for sign, first in ((1, 0), (-1, block // 2)):
            lax.fori_loop(0, tiles // 2, functools.partial(body, sign, first), 0)
        return
    each = tiles // len(beside)
    for k, step in enumerate(beside):
        step()
        for t in range(k * each, (k + 1) * each):
            tile(1 if 2 * t < tiles else -1, pl.ds(t * 8, 8), pl.ds(block + t * 8, 8))


def invert(table, block, spec_ref, store):
    count, _, width = spec_ref.shape
    group = side_by_side(width)

    def step(j):
        parts = [spec_ref[j + u] for u in range(group)]
        both = inverse_dft(table, jnp.concatenate(parts, 1) if group > 1 else parts[0])
        for u in range(group):
            store(j + u, both[:, u * width : (u + 1) * width])

    return [functools.partial(step, j) for j in range(0, count, group)]


def run(steps):
    for step in steps:
        step()


def half_of(ref, rows, half):
    def load(j):
        return jnp.concatenate([ref[2 * j + u, pl.ds(half * rows, rows), :] for u in range(2)], 0)

    return load


def both_grads(block, loads, stores, refs):
    forward, inverse, grad_spec, value_spec, spec, tap_spec, tap_sum = refs
    (ready_grad, load_grad), (ready_value, load_value), (ready_taps, load_taps) = loads
    ready_taps()
    run(spectra(forward, block, load_taps, tap_spec))
    ready_grad()
    run(spectra(forward, block, load_grad, grad_spec))
    ready_value()
    value_steps = spectra(forward, block, load_value, value_spec)
    grad_steps = invert(inverse, block, spec, stores[0])
    if len(value_steps) > 8:
        run(value_steps)
        value_steps = ()
    correlate(block, tap_spec, grad_spec, spec, value_steps)
    if len(grad_steps) > 8:
        run(grad_steps)
        grad_steps = ()
    correlate(block, value_spec, grad_spec, tap_sum, grad_steps)
    run(invert(inverse, block, tap_sum, stores[1]))


def plain_kernel(block, sent_ref, taps_ref, forward, inverse, grad_ref, tap_grad_ref, *refs):
    rows = block // 2

    loads = (
        (tuple, half_of(sent_ref, rows, 0)),
        (tuple, half_of(sent_ref, rows, 1)),
        (tuple, lambda j: taps_ref[pl.ds(j * block, block), :]),
    )

    def store_grad(j, result):
        for u in range(2):
            grad_ref[2 * j + u] = result[u * rows : (u + 1) * rows].astype(BF16)

    def store_taps(j, result):
        tap_grad_ref[pl.ds(j * block, block), :] = result.astype(BF16)

    both_grads(block, loads, (store_grad, store_taps), (forward, inverse, *refs))


def traded(top, bottom):
    half = top.shape[1] // 2
    left = lax.broadcasted_iota(jnp.int32, top.shape, 1) < half
    return (
        jnp.where(left, top, pltpu.roll(bottom, half, 1)),
        jnp.where(left, pltpu.roll(top, half, 1), bottom),
    )


def pack_kernel(grad_ref, value_ref, taps_ref, out_ref):
    half = grad_ref.shape[0] // 2
    own, size = out_ref.shape[2], taps_ref.shape[2]
    for i in range(out_ref.shape[0] // 2):
        columns = pl.ds(i * own, own)
        for n, ref in enumerate((grad_ref, value_ref)):
            pair = traded(ref[pl.ds(0, half), columns], ref[pl.ds(half, half), columns])
            for j in range(2):
                out_ref[2 * i + j, pl.ds(n * half, half), :] = pair[j]
        pair = traded(taps_ref[0, i], taps_ref[1, i])
        for j in range(2):
            out_ref[2 * i + j, pl.ds(2 * half, size), :] = pair[j]


def paired_kernel(sizes, sent_ref, forward, inverse, out_ref, whole, taps, *refs):
    block, size, tap_segs = sizes
    rows, half = block // 2, block // 4
    count = sent_ref.shape[0] // 2

    def untrade(n):
        for i in range(count):
            pair = [sent_ref[2 * i + j, pl.ds(n * half, half), :] for j in range(2)]
            for u, part in enumerate(traded(*pair)):
                whole[n, pl.ds(i * rows + u * half, half), :] = part

    def gather_taps():
        for i in range(count):
            for j in range(2):
                taps[j, pl.ds(i * size, size), :] = sent_ref[2 * i + j, pl.ds(2 * half, size), :].astype(F32)

    loads = (
        (functools.partial(untrade, 0), lambda j: whole[0, pl.ds(j * block, block), :]),
        (functools.partial(untrade, 1), lambda j: whole[1, pl.ds(j * block, block), :]),
        (gather_taps, lambda j: jnp.concatenate([taps[segment(2 * j + u)].astype(BF16) for u in range(2)], 0)),
    )

    def segment(s):
        return s // tap_segs, pl.ds(s % tap_segs, rows, stride=tap_segs), slice(None)

    def store_grad(j, result):
        result = result.astype(BF16)
        for u in range(2):
            at = u * rows
            pair = traded(result[at : at + half], result[at + half : at + rows])
            for side in range(2):
                out_ref[2 * (2 * j + u) + side, pl.ds(0, half), :] = pair[side]

    def store_taps(j, result):
        for u in range(2):
            taps[segment(2 * j + u)] = result[u * rows : (u + 1) * rows]
        if (2 * j + 2) % tap_segs:
            return
        side = 2 * j // tap_segs
        for i in range(count):
            out_ref[2 * i + side, pl.ds(half, size), :] = taps[side, pl.ds(i * size, size), :].astype(BF16)

    both_grads(block, loads, (store_grad, store_taps), (forward, inverse, *refs))


def unpack_kernel(back_ref, grad_ref, taps_ref):
    rows, width = grad_ref.shape
    half, own = rows // 2, back_ref.shape[2]
    tap_rows, tap_segs = taps_ref.shape[:2]
    size = tap_rows * tap_segs
    for i in range(back_ref.shape[0] // 2):
        pair = traded(*[back_ref[2 * i + j, pl.ds(0, half), :] for j in range(2)])
        for u in range(2):
            grad_ref[pl.ds(u * half, half), pl.ds(i * own, own)] = pair[u]
        pair = traded(*[back_ref[2 * i + j, pl.ds(half, size), :] for j in range(2)])
        for side in range(2):
            taps_ref[:, :, pl.ds(side * width + i * own, own)] = pair[side].astype(F32).reshape(tap_rows, tap_segs, own)


def split_kernel(*refs):
    ins, out_ref = refs[:-1], refs[-1]
    count, size, own = out_ref.shape
    rows = size // len(ins)
    for k in range(count):
        for n, ref in enumerate(ins):
            out_ref[k, pl.ds(n * rows, rows), :] = ref[:, k * own : (k + 1) * own]


def call_kernel(body, out_shape, operands, scratch=(), flops=0, far=(), sems=0):
    held = [a for k, a in enumerate(operands) if k not in far]
    held += list(out_shape) + list(scratch)
    padded = sum(int(np.prod(a.shape[:-1])) * max(a.shape[-1], 128) * a.dtype.itemsize for a in held)
    moved = sum(int(np.prod(a.shape)) * a.dtype.itemsize for a in list(operands) + list(out_shape))
    near, away = pl.BlockSpec(memory_space=pltpu.VMEM), pl.BlockSpec(memory_space=pl.ANY)
    scratch_shapes = [pltpu.VMEM(a.shape, a.dtype) for a in scratch]
    if sems:
        scratch_shapes.append(pltpu.SemaphoreType.DMA((sems,)))
    return pl.pallas_call(
        body,
        out_shape=out_shape,
        in_specs=[away if k in far else near for k in range(len(operands))],
        out_specs=[near] * len(out_shape),
        scratch_shapes=scratch_shapes,
        compiler_params=pltpu.CompilerParams(vmem_limit_bytes=min(padded + (6 << 20), 56 << 20)),
        cost_estimate=pl.CostEstimate(flops=flops, bytes_accessed=moved, transcendentals=0),
    )(*operands)


def shards(grad_out, inputs, filter_taps):
    rows, width = grad_out.shape
    ctx, ch = lax.axis_size("ctx"), lax.axis_size("ch")
    tap_rows, tap_segs, channels = filter_taps.shape
    own = width // ctx
    block = 2 * rows
    taps = rows * tap_segs * ch
    size = tap_rows * tap_segs
    blocks, tap_blocks = rows * ctx // block, taps // block
    shape = jax.ShapeDtypeStruct
    paired = own == 128 and ch == 2 and rows % 32 == 0 and size % 16 == 0 and tap_segs % 2 == 0

    forward, inverse = (jnp.asarray(t) for t in dft_tables(block))
    spec = shape((blocks, 2 * block, own), F32)
    tap_spec = shape((tap_blocks, 2 * block, own), F32)
    scratch = [spec, spec, spec, tap_spec, tap_spec]
    flops = 4 * block * block * own * 5 * (blocks + tap_blocks)
    tap_parts = filter_taps.reshape(tap_rows, tap_segs, ch, ctx, own)

    if paired:
        tap_parts = tap_parts.transpose(2, 3, 0, 1, 4).reshape(ch, ctx, size, own)
        (sent,) = call_kernel(
            pack_kernel, [shape((ctx * ch, rows + size, own), BF16)], (grad_out, inputs, tap_parts)
        )
        sent = lax.all_to_all(sent, ("ctx", "ch"), 0, 0, tiled=True)
        (back,) = call_kernel(
            functools.partial(paired_kernel, (block, size, tap_segs)),
            [shape((ctx * ch, rows // 2 + size, own), BF16)],
            (sent, forward, inverse),
            [shape((2, rows * ctx, own), BF16), shape((ch, rows * tap_segs, own), F32)] + scratch,
            flops,
        )
        back = lax.all_to_all(back, ("ctx", "ch"), 0, 0, tiled=True)
        return call_kernel(
            unpack_kernel,
            [shape((rows, width), BF16), shape(filter_taps.shape, F32)],
            (back,),
        )

    (sent,) = call_kernel(split_kernel, [shape((ctx, 2 * rows, own), BF16)], (grad_out, inputs))
    sent = lax.all_to_all(sent, "ctx", 0, 0, tiled=True)
    tap_parts = tap_parts.transpose(3, 2, 0, 1, 4).reshape(ctx * ch, tap_rows, tap_segs, own)
    tap_parts = lax.all_to_all(tap_parts, ("ctx", "ch"), 0, 0, tiled=True)
    tap_all = tap_parts.reshape(ctx, ch, tap_rows, tap_segs, own).transpose(1, 3, 0, 2, 4)
    input_grad, tap_grad = call_kernel(
        functools.partial(plain_kernel, block),
        [shape((ctx, rows, own), BF16), shape((taps, own), BF16)],
        (sent, tap_all.reshape(taps, own), forward, inverse),
        scratch,
        flops,
    )
    back = lax.all_to_all(input_grad, "ctx", 0, 0, tiled=True)
    grad_inputs = back.transpose(1, 0, 2).reshape(rows, width)
    out_parts = tap_grad.reshape(ch, tap_segs, ctx, tap_rows, own).transpose(2, 0, 3, 1, 4)
    out_parts = out_parts.reshape(ctx * ch, tap_rows, tap_segs, own)
    out_parts = lax.all_to_all(out_parts, ("ctx", "ch"), 0, 0, tiled=True)
    out_parts = out_parts.reshape(ctx, ch, tap_rows, tap_segs, own).transpose(2, 3, 1, 0, 4)
    grad_taps = out_parts.reshape(tap_rows, tap_segs, channels).astype(F32)
    return grad_inputs, grad_taps


def solution(mesh):
    return jax.shard_map(
        shards,
        mesh=mesh,
        in_specs=(P("ctx", "ch"), P("ctx", "ch"), P("ctx", "ch", None)),
        out_specs=(P("ctx", "ch"), P("ctx", "ch", None)),
        check_vma=False,
    )
```

```python
import functools
import math

import jax
import jax.numpy as jnp
import numpy as np
from jax import lax
from jax.experimental import pallas as pl
from jax.experimental.pallas import tpu as pltpu
from jax.sharding import PartitionSpec as P

F32 = jnp.float32
BF16 = jnp.bfloat16


def two_bf16(table):
    upper = table.astype(np.float32).astype(jnp.bfloat16)
    lower = (table - upper.astype(np.float64)).astype(np.float32).astype(jnp.bfloat16)
    return np.stack([upper, lower])


def dft_tables(block):
    freq = np.concatenate([np.arange(0, block, 2), np.arange(1, block, 2)])
    turns = ((2 * freq[:, None] + 1) * np.arange(block)[None, :]) % (4 * block)
    angle = turns * (np.pi / (2 * block))
    forward = np.concatenate([np.cos(angle), -np.sin(angle)], 0)
    return two_bf16(forward), (forward.T / block).astype(np.float32).astype(jnp.bfloat16)


def forward_dft(table, columns):
    first = jnp.dot(table[0], columns, preferred_element_type=F32)
    return first + jnp.dot(table[1], columns, preferred_element_type=F32)


def inverse_dft(table, spec):
    return jnp.dot(table[...], spec.astype(BF16), preferred_element_type=F32)


def side_by_side(width):
    return 2 if width % 128 == 0 else 1


def spectra(table, block, load, spec_ref):
    count, _, width = spec_ref.shape
    group = side_by_side(width)

    def step(j):
        parts = [load(j + u) for u in range(group)]
        both = forward_dft(table, jnp.concatenate(parts, 1) if group > 1 else parts[0])
        for u in range(group):
            spec_ref[j + u] = both[:, u * width : (u + 1) * width]

    return [functools.partial(step, j) for j in range(0, count, group)]


def correlate(block, left_ref, grad_ref, out_ref, beside=()):
    lefts, outs, count = left_ref.shape[0], out_ref.shape[0], grad_ref.shape[0]
    tiles = block // 8

    def pieces(ref, real, imag):
        return [(ref[j, real], ref[j, imag]) for j in range(ref.shape[0])]

    def tile(sign, real, imag):
        grad, left = pieces(grad_ref, real, imag), pieces(left_ref, real, imag)
        window = []
        for j in range(count):
            re, im = grad[j]
            if j + 1 < count:
                next_re, next_im = grad[j + 1]
                re, im = (re + next_im, im - next_re) if sign > 0 else (re - next_im, im + next_re)
            window.append((re, im, re + im))
        left = [(re, im, re - im) for re, im in left]
        for a in range(outs):
            terms = [[l * w for l, w in zip(*pair)] for pair in zip(left, window[a:])]
            reals, imags, mixed = (functools.reduce(lambda x, y: x + y, column) for column in zip(*terms))
            out_ref[a, real], out_ref[a, imag] = reals + imags, mixed - (reals - imags)

    def body(sign, first, t, carry):
        at = pl.multiple_of(first + t * 8, 8)
        tile(sign, pl.ds(at, 8), pl.ds(pl.multiple_of(block + at, 8), 8))
        return carry

    if not beside:
        for sign, first in ((1, 0), (-1, block // 2)):
            lax.fori_loop(0, tiles // 2, functools.partial(body, sign, first), 0)
        return
    each = tiles // len(beside)
    for k, step in enumerate(beside):
        step()
        for t in range(k * each, (k + 1) * each):
            tile(1 if 2 * t < tiles else -1, pl.ds(t * 8, 8), pl.ds(block + t * 8, 8))


def invert(table, block, spec_ref, store):
    count, _, width = spec_ref.shape
    group = side_by_side(width)

    def step(j):
        parts = [spec_ref[j + u] for u in range(group)]
        both = inverse_dft(table, jnp.concatenate(parts, 1) if group > 1 else parts[0])
        for u in range(group):
            store(j + u, both[:, u * width : (u + 1) * width])

    return [functools.partial(step, j) for j in range(0, count, group)]


def run(steps):
    for step in steps:
        step()


def half_of(ref, rows, half):
    def load(j):
        return jnp.concatenate([ref[2 * j + u, pl.ds(half * rows, rows), :] for u in range(2)], 0)

    return load


def both_grads(block, loads, stores, refs):
    forward, inverse, grad_spec, value_spec, spec, tap_spec, tap_sum = refs
    (ready_grad, load_grad), (ready_value, load_value), (ready_taps, load_taps) = loads
    ready_taps()
    run(spectra(forward, block, load_taps, tap_spec))
    ready_grad()
    run(spectra(forward, block, load_grad, grad_spec))
    ready_value()
    value_steps = spectra(forward, block, load_value, value_spec)
    grad_steps = invert(inverse, block, spec, stores[0])
    if len(value_steps) > 8:
        run(value_steps)
        value_steps = ()
    correlate(block, tap_spec, grad_spec, spec, value_steps)
    if len(grad_steps) > 8:
        run(grad_steps)
        grad_steps = ()
    correlate(block, value_spec, grad_spec, tap_sum, grad_steps)
    run(invert(inverse, block, tap_sum, stores[1]))


def plain_kernel(block, sent_ref, taps_ref, forward, inverse, grad_ref, tap_grad_ref, *refs):
    rows = block // 2

    loads = (
        (tuple, half_of(sent_ref, rows, 0)),
        (tuple, half_of(sent_ref, rows, 1)),
        (tuple, lambda j: taps_ref[pl.ds(j * block, block), :]),
    )

    def store_grad(j, result):
        for u in range(2):
            grad_ref[2 * j + u] = result[u * rows : (u + 1) * rows].astype(BF16)

    def store_taps(j, result):
        tap_grad_ref[pl.ds(j * block, block), :] = result.astype(BF16)

    both_grads(block, loads, (store_grad, store_taps), (forward, inverse, *refs))


def traded(top, bottom):
    half = top.shape[1] // 2
    left = lax.broadcasted_iota(jnp.int32, top.shape, 1) < half
    return (
        jnp.where(left, top, pltpu.roll(bottom, half, 1)),
        jnp.where(left, pltpu.roll(top, half, 1), bottom),
    )


def pack_kernel(grad_ref, value_ref, taps_ref, out_ref):
    half = grad_ref.shape[0] // 2
    own, size = out_ref.shape[2], taps_ref.shape[2]
    for i in range(out_ref.shape[0] // 2):
        columns = pl.ds(i * own, own)
        for n, ref in enumerate((grad_ref, value_ref)):
            pair = traded(ref[pl.ds(0, half), columns], ref[pl.ds(half, half), columns])
            for j in range(2):
                out_ref[2 * i + j, pl.ds(n * half, half), :] = pair[j]
        pair = traded(taps_ref[0, i], taps_ref[1, i])
        for j in range(2):
            out_ref[2 * i + j, pl.ds(2 * half, size), :] = pair[j]


def paired_kernel(sizes, sent_ref, forward, inverse, out_ref, whole, taps, *refs):
    block, size, tap_segs = sizes
    rows, half = block // 2, block // 4
    count = sent_ref.shape[0] // 2

    def untrade(n):
        for i in range(count):
            pair = [sent_ref[2 * i + j, pl.ds(n * half, half), :] for j in range(2)]
            for u, part in enumerate(traded(*pair)):
                whole[n, pl.ds(i * rows + u * half, half), :] = part

    def gather_taps():
        for i in range(count):
            for j in range(2):
                taps[j, pl.ds(i * size, size), :] = sent_ref[2 * i + j, pl.ds(2 * half, size), :].astype(F32)

    loads = (
        (functools.partial(untrade, 0), lambda j: whole[0, pl.ds(j * block, block), :]),
        (functools.partial(untrade, 1), lambda j: whole[1, pl.ds(j * block, block), :]),
        (gather_taps, lambda j: jnp.concatenate([taps[segment(2 * j + u)].astype(BF16) for u in range(2)], 0)),
    )

    def segment(s):
        return s // tap_segs, pl.ds(s % tap_segs, rows, stride=tap_segs), slice(None)

    def store_grad(j, result):
        result = result.astype(BF16)
        for u in range(2):
            at = u * rows
            pair = traded(result[at : at + half], result[at + half : at + rows])
            for side in range(2):
                out_ref[2 * (2 * j + u) + side, pl.ds(0, half), :] = pair[side]

    def store_taps(j, result):
        for u in range(2):
            taps[segment(2 * j + u)] = result[u * rows : (u + 1) * rows]
        if (2 * j + 2) % tap_segs:
            return
        side = 2 * j // tap_segs
        for i in range(count):
            out_ref[2 * i + side, pl.ds(half, size), :] = taps[side, pl.ds(i * size, size), :].astype(BF16)

    both_grads(block, loads, (store_grad, store_taps), (forward, inverse, *refs))


def unpack_kernel(parts, back_ref, grad_hbm, taps_hbm, grad_ref, taps_ref, sems):
    rows, width = grad_ref.shape
    half, own = rows // 2, back_ref.shape[2]
    tap_rows, tap_segs = taps_ref.shape[:2]
    size = tap_rows * tap_segs
    each = back_ref.shape[0] // 2 // parts
    copies = []

    def leave(near, far, columns):
        copies.append(pltpu.make_async_copy(near.at[..., columns], far.at[..., columns], sems.at[len(copies)]))
        copies[-1].start()

    for n in range(parts):
        for i in range(n * each, (n + 1) * each):
            pair = traded(*[back_ref[2 * i + j, pl.ds(0, half), :] for j in range(2)])
            for u in range(2):
                grad_ref[pl.ds(u * half, half), pl.ds(i * own, own)] = pair[u]
            pair = traded(*[back_ref[2 * i + j, pl.ds(half, size), :] for j in range(2)])
            for side in range(2):
                tap_part = pair[side].astype(F32).reshape(tap_rows, tap_segs, own)
                taps_ref[:, :, pl.ds(side * width + i * own, own)] = tap_part
        leave(grad_ref, grad_hbm, pl.ds(n * each * own, each * own))
        for side in range(2):
            leave(taps_ref, taps_hbm, pl.ds(side * width + n * each * own, each * own))
    for copy in copies:
        copy.wait()


def split_kernel(*refs):
    ins, out_ref = refs[:-1], refs[-1]
    count, size, own = out_ref.shape
    rows = size // len(ins)
    for k in range(count):
        for n, ref in enumerate(ins):
            out_ref[k, pl.ds(n * rows, rows), :] = ref[:, k * own : (k + 1) * own]


def call_kernel(body, out_shape, operands, scratch=(), flops=0, far_out=(), sems=0):
    held = list(operands) + [a for k, a in enumerate(out_shape) if k not in far_out] + list(scratch)
    padded = sum(int(np.prod(a.shape[:-1])) * max(a.shape[-1], 128) * a.dtype.itemsize for a in held)
    moved = sum(int(np.prod(a.shape)) * a.dtype.itemsize for a in list(operands) + list(out_shape))
    near, away = pl.BlockSpec(memory_space=pltpu.VMEM), pl.BlockSpec(memory_space=pl.ANY)
    scratch_shapes = [pltpu.VMEM(a.shape, a.dtype) for a in scratch]
    if sems:
        scratch_shapes.append(pltpu.SemaphoreType.DMA((sems,)))
    return pl.pallas_call(
        body,
        out_shape=out_shape,
        in_specs=[near] * len(operands),
        out_specs=[away if k in far_out else near for k in range(len(out_shape))],
        scratch_shapes=scratch_shapes,
        compiler_params=pltpu.CompilerParams(vmem_limit_bytes=min(padded + (6 << 20), 56 << 20)),
        cost_estimate=pl.CostEstimate(flops=flops, bytes_accessed=moved, transcendentals=0),
    )(*operands)


def shards(grad_out, inputs, filter_taps):
    rows, width = grad_out.shape
    ctx, ch = lax.axis_size("ctx"), lax.axis_size("ch")
    tap_rows, tap_segs, channels = filter_taps.shape
    own = width // ctx
    block = 2 * rows
    taps = rows * tap_segs * ch
    size = tap_rows * tap_segs
    blocks, tap_blocks = rows * ctx // block, taps // block
    shape = jax.ShapeDtypeStruct
    paired = own == 128 and ch == 2 and rows % 32 == 0 and size % 16 == 0 and tap_segs % 2 == 0

    forward, inverse = (jnp.asarray(t) for t in dft_tables(block))
    spec = shape((blocks, 2 * block, own), F32)
    tap_spec = shape((tap_blocks, 2 * block, own), F32)
    scratch = [spec, spec, spec, tap_spec, tap_spec]
    flops = 4 * block * block * own * 5 * (blocks + tap_blocks)
    tap_parts = filter_taps.reshape(tap_rows, tap_segs, ch, ctx, own)

    if paired:
        tap_parts = tap_parts.transpose(2, 3, 0, 1, 4).reshape(ch, ctx, size, own)
        (sent,) = call_kernel(
            pack_kernel, [shape((ctx * ch, rows + size, own), BF16)], (grad_out, inputs, tap_parts)
        )
        sent = lax.all_to_all(sent, ("ctx", "ch"), 0, 0, tiled=True)
        (back,) = call_kernel(
            functools.partial(paired_kernel, (block, size, tap_segs)),
            [shape((ctx * ch, rows // 2 + size, own), BF16)],
            (sent, forward, inverse),
            [shape((2, rows * ctx, own), BF16), shape((ch, rows * tap_segs, own), F32)] + scratch,
            flops,
        )
        back = lax.all_to_all(back, ("ctx", "ch"), 0, 0, tiled=True)
        outs = [shape((rows, width), BF16), shape(filter_taps.shape, F32)]
        parts = math.gcd(ctx, 4)
        return call_kernel(
            functools.partial(unpack_kernel, parts), outs, (back,), outs, far_out=(0, 1), sems=3 * parts
        )

    (sent,) = call_kernel(split_kernel, [shape((ctx, 2 * rows, own), BF16)], (grad_out, inputs))
    sent = lax.all_to_all(sent, "ctx", 0, 0, tiled=True)
    tap_parts = tap_parts.transpose(3, 2, 0, 1, 4).reshape(ctx * ch, tap_rows, tap_segs, own)
    tap_parts = lax.all_to_all(tap_parts, ("ctx", "ch"), 0, 0, tiled=True)
    tap_all = tap_parts.reshape(ctx, ch, tap_rows, tap_segs, own).transpose(1, 3, 0, 2, 4)
    input_grad, tap_grad = call_kernel(
        functools.partial(plain_kernel, block),
        [shape((ctx, rows, own), BF16), shape((taps, own), BF16)],
        (sent, tap_all.reshape(taps, own), forward, inverse),
        scratch,
        flops,
    )
    back = lax.all_to_all(input_grad, "ctx", 0, 0, tiled=True)
    grad_inputs = back.transpose(1, 0, 2).reshape(rows, width)
    out_parts = tap_grad.reshape(ch, tap_segs, ctx, tap_rows, own).transpose(2, 0, 3, 1, 4)
    out_parts = out_parts.reshape(ctx * ch, tap_rows, tap_segs, own)
    out_parts = lax.all_to_all(out_parts, ("ctx", "ch"), 0, 0, tiled=True)
    out_parts = out_parts.reshape(ctx, ch, tap_rows, tap_segs, own).transpose(2, 3, 1, 0, 4)
    grad_taps = out_parts.reshape(tap_rows, tap_segs, channels).astype(F32)
    return grad_inputs, grad_taps


def solution(mesh):
    return jax.shard_map(
        shards,
        mesh=mesh,
        in_specs=(P("ctx", "ch"), P("ctx", "ch"), P("ctx", "ch", None)),
        out_specs=(P("ctx", "ch"), P("ctx", "ch", None)),
        check_vma=False,
    )
```
